32 devices in a mesh: fsdp: 16 (over z, y, core), tp: 2 (over x).
Axes of the slice: x: 2, y: 2, z: 4, core: 2. Of those that a mesh axis runs over, the one named last changes fastest.
Arguments:
- patches: bfloat16 [7168, 3072], P('fsdp'), may hold values from -500 to 500
- cotangent: bfloat16 [7168, 3072], P('fsdp'), may hold values from -6 to 6
- counts: int32 [16, 4], replicated, may hold values from 32 to 112, as said below
- masks: int32 [4], replicated, may hold values from 0 to 15, as said below
- norm_gain: float32 [3072], replicated, may hold values from 0.25 to 1.75
- qk_gain: float32 [2, 128], replicated, may hold values from 0.25 to 1.75
- qkv_weight: bfloat16 [3072, 9216], P('fsdp', 'tp'), may hold values from -0.109375 to 0.109375
- out_weight: bfloat16 [3072, 3072], P('fsdp', 'tp'), may hold values from -0.109375 to 0.109375
Outputs:
- attended: bfloat16 [7168, 3072], P('fsdp', 'tp')
- grad_rows: bfloat16 [7168, 3072], P('fsdp', 'tp')
- grad_qkv_weight: float32 [3072, 9216], P('fsdp', 'tp')
- grad_out_weight: float32 [3072, 3072], P('fsdp', 'tp')
The draws below stay inside these ranges and needn't reach their ends.
Inputs may be any that keep to these rules, and one draw needn't show every extreme that they name: `masks`: in every draw some slot's mask is 15. `counts`: in every draw some run block holds 112 patches in each of its slots.
All inputs are finite; a program needn't handle non-finite values.
Results may differ from the reference program's by a relative error of at most 0.02.
Values may be sent and summed in bfloat16 or wider, within the bound.
No kernel may reach another device: no remote copies, remote signals or barrier semaphores. Data moves between devices by JAX's collectives and lax.ppermute only.
A program may use at most 192 MiB of HBM per device.

```python
import math
import jax
import jax.numpy as jnp
from jax import lax

D = 3072
HEADS = 24
HD = 128
CAP = 112
IMGS = 4
PMIN = 32
TOK = 448
TOKENS = 7168
N_FSDP = 16
N_TP = 2


def plan_helper(key):
    masks = jax.random.randint(jax.random.fold_in(key, 11), (IMGS,), 0, N_FSDP).astype(jnp.int32)
    widest = jax.random.randint(jax.random.fold_in(key, 17), (), 0, IMGS)
    masks = jnp.where(jnp.arange(IMGS, dtype=jnp.int32) == widest, N_FSDP - 1, masks).astype(jnp.int32)
    full_replica = jax.random.randint(jax.random.fold_in(key, 14), (), 0, N_FSDP)
    return (masks, full_replica)


def draw_masks(key, part):
    masks, full_replica = plan_helper(key)
    return masks


def draw_counts(key, part):
    masks, full_replica = plan_helper(key)
    key = jax.random.fold_in(key, 3)
    counts = jax.random.randint(key, (N_FSDP, IMGS), PMIN, CAP + 1)
    full_sources = jnp.bitwise_xor(full_replica, masks)
    replica_ids = jnp.arange(N_FSDP, dtype=jnp.int32)
    is_full = replica_ids[:, None] == full_sources[None, :]
    return jnp.where(is_full, CAP, counts).astype(jnp.int32)


def draw_patches(key, part):
    key = jax.random.fold_in(key, 5)
    base_key, row_key, col_key = jax.random.split(key, 3)
    row_scale = jnp.exp(jax.random.uniform(row_key, (TOKENS, 1), jnp.float32, 0.0, math.log(10.0)))
    col_scale = jnp.exp(jax.random.uniform(col_key, (1, D), jnp.float32, 0.0, math.log(10.0)))
    base = jnp.clip(jax.random.normal(base_key, (TOKENS, D), jnp.float32), -5.0, 5.0)
    return (base * row_scale * col_scale).astype(jnp.bfloat16)


def block_levels(own_key, dims, shards, least, top_value):
    gain = 1.0
    for axis_at, parts in shards:
        heights = jax.random.uniform(jax.random.fold_in(jax.random.fold_in(own_key, 6), axis_at), (parts,), jnp.float32, least / len(shards), top_value / len(shards))
        gain = gain * jnp.repeat(jnp.exp(heights), dims[axis_at] // parts).reshape((-1,) + (1,) * (len(dims) - 1 - axis_at))
    return gain


def gaussian(rng, shape, width, reach, pieces=(), kind=jnp.bfloat16):
    loudness = block_levels(rng, shape, pieces, -0.22, 0.18) if pieces else 1.0
    drawn = jax.random.normal(rng, shape, jnp.float32) * width * loudness
    return jnp.minimum(jnp.maximum(drawn, -reach), reach).astype(kind)


def setup_inputs(seed: int = 0) -> dict:
    key_of = jax.random.split(jax.random.key(seed), 9)
    return {
        "patches": draw_patches(jax.random.fold_in(key_of[8], 71), 0),
        "cotangent": gaussian(key_of[1], (TOKENS, D), 1.0, 6.0, ((0, 16),)),
        "counts": draw_counts(jax.random.fold_in(key_of[8], 71), 0),
        "masks": draw_masks(jax.random.fold_in(key_of[8], 71), 0),
        "norm_gain": jnp.clip(1.0 + 0.15 * jax.random.normal(key_of[4], (D,), jnp.float32), 0.25, 1.75),
        "qk_gain": jnp.clip(1.0 + 0.15 * jax.random.normal(key_of[5], (2, HD), jnp.float32), 0.25, 1.75),
        "qkv_weight": gaussian(key_of[6], (D, 3 * HEADS * HD), D ** -0.5, 0.109375, ((0, 16), (1, 2))),
        "out_weight": gaussian(key_of[7], (D, HEADS * HD), (HEADS * HD) ** -0.5, 0.109375, ((0, 16), (1, 2))),
    }


epsilon = 1e-06

def norm_rows(values):
    row_mean = lax.optimization_barrier(jnp.mean(values, axis=-1, keepdims=True))
    centred = values - row_mean
    factor = lax.rsqrt(lax.optimization_barrier(jnp.mean(centred * centred, axis=-1, keepdims=True)) + epsilon)
    return (centred * factor, factor)

def norm_back(upstream, normed, factor):
    return factor * (upstream - lax.optimization_barrier(jnp.mean(upstream, axis=-1, keepdims=True)) - normed * lax.optimization_barrier(jnp.mean(upstream * normed, axis=-1, keepdims=True)))

def group_sum(left_rows, right_rows):
    left_groups = left_rows.reshape(left_rows.shape[0], N_TP, -1).astype(jnp.float32)
    right_groups = right_rows.reshape(right_rows.shape[0], N_TP, -1).astype(jnp.float32)
    partial_value = jnp.einsum('tgc,dgc->gtd', left_groups, right_groups)
    rounded = lax.optimization_barrier(partial_value.astype(jnp.bfloat16))
    return lax.optimization_barrier(jnp.sum(rounded.astype(jnp.float32), axis=0))

def one_replica(block_rows, live_slots, upstream_rows, norm_gain, qk_gain, qkv_weight, out_weight):
    is_live = live_slots.reshape(TOK)
    allowed = live_slots[:, :, None] & live_slots[:, None, :] | jnp.eye(CAP, dtype=bool)[None]
    centred_rows, row_factor = norm_rows(block_rows.astype(jnp.float32))
    normed = (centred_rows * norm_gain.astype(jnp.float32)).astype(jnp.bfloat16)
    projected = jnp.dot(normed, qkv_weight, preferred_element_type=jnp.float32).reshape(IMGS, CAP, HEADS, 3, HD)
    query_hat, query_factor = norm_rows(projected[:, :, :, 0])
    key_hat, key_factor = norm_rows(projected[:, :, :, 1])
    query_scale = qk_gain[0].astype(jnp.float32) * HD ** (-0.5)
    key_scale = qk_gain[1].astype(jnp.float32)
    query = (query_hat * query_scale).astype(jnp.bfloat16)
    key_rows = (key_hat * key_scale).astype(jnp.bfloat16)
    values = projected[:, :, :, 2].astype(jnp.bfloat16)
    scores = jnp.einsum('sqhe,skhe->shqk', query.astype(jnp.float32), key_rows.astype(jnp.float32))
    raised = jnp.where(allowed[:, None], jnp.exp(scores), 0.0)
    attention = raised / lax.optimization_barrier(jnp.sum(raised, axis=-1, keepdims=True))
    rounded_attention = attention.astype(jnp.bfloat16)
    mixed = jnp.einsum('shqk,skhe->sqhe', rounded_attention.astype(jnp.float32), values.astype(jnp.float32))
    mixed = mixed.astype(jnp.bfloat16).reshape(TOK, HEADS * HD)
    attended = jnp.where(is_live[:, None], group_sum(mixed, out_weight), 0.0).astype(jnp.bfloat16)
    upstream_rows = jnp.where(is_live[:, None], upstream_rows, jnp.zeros((), jnp.bfloat16))
    grad_mixed = jnp.dot(upstream_rows, out_weight, preferred_element_type=jnp.float32).astype(jnp.bfloat16)
    grad_heads = grad_mixed.reshape(IMGS, CAP, HEADS, HD).astype(jnp.float32)
    grad_value = jnp.einsum('shqk,sqhe->skhe', rounded_attention.astype(jnp.float32), grad_heads)
    grad_attention = jnp.einsum('sqhe,skhe->shqk', grad_heads, values.astype(jnp.float32))
    grad_scores = attention * (grad_attention - lax.optimization_barrier(jnp.sum(attention * grad_attention, axis=-1, keepdims=True)))
    grad_scores = grad_scores.astype(jnp.bfloat16).astype(jnp.float32)
    grad_query = jnp.einsum('shqk,skhe->sqhe', grad_scores, key_rows.astype(jnp.float32))
    grad_key = jnp.einsum('shqk,sqhe->skhe', grad_scores, query.astype(jnp.float32))
    query_grad = norm_back(grad_query * query_scale, query_hat, query_factor)
    key_grad = norm_back(grad_key * key_scale, key_hat, key_factor)
    grad_qkv = jnp.stack([query_grad, key_grad, grad_value], axis=3).astype(jnp.bfloat16).reshape(TOK, 3 * HEADS * HD)
    qkv_term = lax.dot_general(normed, grad_qkv, (((0,), (0,)), ((), ())), preferred_element_type=jnp.float32).astype(jnp.bfloat16)
    out_term = lax.dot_general(upstream_rows, mixed, (((0,), (0,)), ((), ())), preferred_element_type=jnp.float32).astype(jnp.bfloat16)
    grad_normed = group_sum(grad_qkv, qkv_weight)
    grad_rows = norm_back(grad_normed * norm_gain.astype(jnp.float32), centred_rows, row_factor).astype(jnp.bfloat16)
    return (attended, grad_rows, qkv_term, out_term)

def reference(patches, cotangent, counts, masks, norm_gain, qk_gain, qkv_weight, out_weight):
    slot_ids = jnp.arange(IMGS, dtype=jnp.int32)
    places = jnp.arange(CAP, dtype=jnp.int32)
    replicas = jnp.arange(N_FSDP, dtype=jnp.int32)
    slotted = patches.reshape(N_FSDP, IMGS, CAP, D)

    def replica_step(carry, target):
        sources = jnp.bitwise_xor(target, masks).astype(jnp.int32)
        run_counts = lax.optimization_barrier(jnp.sum(jnp.where(replicas[:, None] == sources[None, :], counts, 0), axis=0)).astype(jnp.int32)
        live_slots = places[None, :] < run_counts[:, None]
        picked = slotted[sources, slot_ids]
        block_rows = jnp.where(live_slots[:, :, None], picked, jnp.zeros((), jnp.bfloat16)).reshape(TOK, D)
        upstream_rows = lax.dynamic_slice_in_dim(cotangent, (target * TOK).astype(jnp.int32), TOK, 0)
        attended, grad_rows, qkv_term, out_term = one_replica(block_rows, live_slots, upstream_rows, norm_gain, qk_gain, qkv_weight, out_weight)
        return ((carry[0] + qkv_term.astype(jnp.float32), carry[1] + out_term.astype(jnp.float32)), (attended, grad_rows))
    initial = (jnp.zeros((D, 3 * HEADS * HD), jnp.float32), jnp.zeros((D, HEADS * HD), jnp.float32))
    (grad_qkv_weight, grad_out_weight), (attended, grad_rows) = lax.scan(replica_step, initial, replicas)
    return (attended.reshape(TOKENS, D), grad_rows.reshape(TOKENS, D), grad_qkv_weight, grad_out_weight)
```

```python
import functools
import jax
import jax.numpy as jnp
from jax import lax
from jax.experimental import pallas as pl
from jax.experimental.pallas import tpu as pltpu
from jax.sharding import PartitionSpec as P

epsilon = 1e-06
PLANE = 4


def partner_2(value, axis, stride):
    mask = 2**stride
    pairs = [(source, source ^ mask) for source in range(lax.axis_size(axis))]
    return lax.ppermute(value, axis, pairs)


def norm_rows(values):
    row_mean = jnp.mean(values, axis=-1, keepdims=True)
    centred = values - row_mean
    factor = lax.rsqrt(jnp.mean(centred * centred, axis=-1, keepdims=True) + epsilon)
    return (centred * factor, factor)


def norm_back(upstream, normed, factor):
    return factor * (
        upstream
        - jnp.mean(upstream, axis=-1, keepdims=True)
        - normed * jnp.mean(upstream * normed, axis=-1, keepdims=True)
    )


def per_device(patches, cotangent, counts, masks, norm_gain, qk_gain, qkv_weight, out_weight):
    replicas = lax.axis_size("fsdp")
    groups = lax.axis_size("tp")
    my_replica = lax.axis_index("fsdp")
    my_group = lax.axis_index("tp")
    tok_rows = patches.shape[0]
    images = counts.shape[1]
    slot_rows = tok_rows // images
    model_width = norm_gain.shape[0]
    share_width = model_width // groups
    head_dim = qk_gain.shape[1]
    qkv_cols = qkv_weight.shape[1]
    out_cols = out_weight.shape[1]
    local_heads = out_cols // head_dim
    row_slot = jnp.arange(tok_rows, dtype=jnp.int32) // slot_rows
    holding = lax.dynamic_slice_in_dim(patches, my_group * share_width, share_width, 1)
    digit_count = replicas.bit_length() - 1
    digit_order = list(range(digit_count))
    for bit_place in digit_order:
        partner = partner_2(holding, "fsdp", bit_place)
        moving = jnp.bitwise_and(jnp.right_shift(masks, bit_place), 1) == 1
        take_rows = jnp.take(moving, row_slot)
        holding = jnp.where(take_rows[:, None], partner, holding)
    replica_ids = jnp.arange(replicas, dtype=jnp.int32)
    sources = jnp.bitwise_xor(my_replica, masks)
    run_counts = jnp.sum(jnp.where(replica_ids[:, None] == sources[None, :], counts, 0), axis=0)
    places = jnp.arange(slot_rows, dtype=jnp.int32)
    live_slots = places[None, :] < run_counts[:, None]
    is_live = live_slots.reshape(tok_rows)
    allowed = live_slots[:, :, None] & live_slots[:, None, :] | jnp.eye(slot_rows, dtype=bool)[None]
    packed = jnp.where(is_live[:, None], holding, jnp.zeros((), holding.dtype))
    block_rows = lax.all_gather(packed, "tp", axis=1, tiled=True)
    qkv_full, out_full = (
        lax.all_gather(qkv_weight, "fsdp", axis=0, tiled=True),
        lax.all_gather(out_weight, "fsdp", axis=0, tiled=True),
    )
    centred_rows, row_factor = norm_rows(block_rows.astype(jnp.float32))
    normed = (centred_rows * norm_gain).astype(jnp.bfloat16)
    projected = jnp.dot(normed, qkv_full, preferred_element_type=jnp.float32).reshape(
        images, slot_rows, local_heads, 3, head_dim
    )
    query_hat, query_factor = norm_rows(projected[:, :, :, 0])
    key_hat, key_factor = norm_rows(projected[:, :, :, 1])
    query_scale = qk_gain[0] * head_dim ** (-0.5)
    key_scale = qk_gain[1]
    query = (query_hat * query_scale).astype(jnp.bfloat16)
    key_rows = (key_hat * key_scale).astype(jnp.bfloat16)
    values = projected[:, :, :, 2].astype(jnp.bfloat16)
    scores = jnp.einsum("sqhe,skhe->shqk", query, key_rows, preferred_element_type=jnp.float32)
    raised = jnp.where(allowed[:, None], jnp.exp(scores), 0.0)
    attention = raised / jnp.sum(raised, axis=-1, keepdims=True)
    rounded_attention = attention.astype(jnp.bfloat16)
    mixed = jnp.einsum(
        "shqk,skhe->sqhe", rounded_attention, values, preferred_element_type=jnp.float32
    )
    mixed = mixed.astype(jnp.bfloat16).reshape(tok_rows, out_cols)
    partial_value = lax.dot_general(
        mixed, out_full, (((1,), (1,)), ((), ())), preferred_element_type=jnp.float32
    )
    attended = lax.psum_scatter(
        partial_value.astype(jnp.bfloat16), "tp", scatter_dimension=1, tiled=True
    ).astype(jnp.float32)
    attended = jnp.where(is_live[:, None], attended, 0.0).astype(jnp.bfloat16)
    upstream_rows = jnp.where(is_live[:, None], cotangent, jnp.zeros((), cotangent.dtype))
    grad_mixed = jnp.dot(upstream_rows, out_full, preferred_element_type=jnp.float32).astype(
        jnp.bfloat16
    )
    grad_heads = grad_mixed.reshape(images, slot_rows, local_heads, head_dim)
    grad_value = jnp.einsum(
        "shqk,sqhe->skhe", rounded_attention, grad_heads, preferred_element_type=jnp.float32
    )
    grad_attention = jnp.einsum(
        "sqhe,skhe->shqk", grad_heads, values, preferred_element_type=jnp.float32
    )
    grad_scores = attention * (
        grad_attention - jnp.sum(attention * grad_attention, axis=-1, keepdims=True)
    )
    grad_scores = grad_scores.astype(jnp.bfloat16)
    grad_query = jnp.einsum(
        "shqk,skhe->sqhe", grad_scores, key_rows, preferred_element_type=jnp.float32
    )
    grad_key = jnp.einsum("shqk,sqhe->skhe", grad_scores, query, preferred_element_type=jnp.float32)
    query_grad = norm_back(grad_query * query_scale, query_hat, query_factor)
    key_grad = norm_back(grad_key * key_scale, key_hat, key_factor)
    grad_qkv = (
        jnp.stack([query_grad, key_grad, grad_value], axis=3)
        .astype(jnp.bfloat16)
        .reshape(tok_rows, qkv_cols)
    )
    qkv_term = lax.dot_general(
        normed, grad_qkv, (((0,), (0,)), ((), ())), preferred_element_type=jnp.float32
    )
    out_term = lax.dot_general(
        upstream_rows, mixed, (((0,), (0,)), ((), ())), preferred_element_type=jnp.float32
    )
    stacked = lax.psum_scatter(
        jnp.concatenate([qkv_term, out_term], axis=1).astype(jnp.bfloat16),
        "fsdp",
        scatter_dimension=0,
        tiled=True,
    ).astype(jnp.float32)
    grad_qkv_weight = stacked[:, :qkv_cols]
    grad_out_weight = stacked[:, qkv_cols:]
    partial_back = lax.dot_general(
        grad_qkv, qkv_full, (((1,), (1,)), ((), ())), preferred_element_type=jnp.float32
    )
    summed = lax.psum(partial_back.astype(jnp.bfloat16), "tp").astype(jnp.float32)
    grad_full = norm_back(summed * norm_gain, centred_rows, row_factor)
    grad_share = lax.dynamic_slice_in_dim(grad_full, my_group * share_width, share_width, 1)
    grad_rows = grad_share.astype(jnp.bfloat16)
    return (attended, grad_rows, grad_qkv_weight, grad_out_weight)


def swap_fsdp(value, mask):
    pairs = [(source, source ^ mask) for source in range(lax.axis_size("fsdp"))]
    return lax.ppermute(value, "fsdp", pairs)


def swap_tp(value):
    return lax.ppermute(value, "tp", [(0, 1), (1, 0)])


def shift_planes(value, step, senders):
    pairs = [
        (plane * PLANE + place, (plane + step) * PLANE + place)
        for plane in senders
        for place in range(PLANE)
    ]
    return lax.ppermute(value, "fsdp", pairs)


def after(value, *earlier):
    return lax.optimization_barrier((value,) + earlier)[0]


class PlaneGather:
    def __init__(self, own, planes, my_plane):
        self.own, self.planes, self.my_plane = (own, planes, my_plane)
        self.rights, self.lefts = ([], [])
        self.right = self.left = own

    def step(self, *earlier):
        step = len(self.rights) + 1
        right = after(self.right, *earlier) if earlier else self.right
        left = after(self.left, *earlier) if earlier else self.left
        self.right = shift_planes(right, 1, range(step - 1, self.planes - 1))
        self.left = shift_planes(left, -1, range(1, self.planes - step + 1))
        self.rights.append(self.right)
        self.lefts.append(self.left)

    def last(self):
        return (self.right, self.left)

    def whole(self):
        own, planes, my_plane = (self.own, self.planes, self.my_plane)
        whole = jnp.zeros((planes,) + own.shape, own.dtype)
        whole = lax.dynamic_update_index_in_dim(whole, own, my_plane, 0)
        for step in range(1, planes):
            piece = jnp.where(
                my_plane >= step, self.rights[step - 1], self.lefts[planes - step - 1]
            )
            place = lax.rem(my_plane - step + planes, planes)
            whole = lax.dynamic_update_index_in_dim(whole, piece, place, 0)
        return whole.reshape((planes * own.shape[0],) + own.shape[1:])


def add_rounded(left, right):
    return (left.astype(jnp.float32) + right.astype(jnp.float32)).astype(jnp.bfloat16)


class PlaneReduce:
    def __init__(self, terms, planes, my_plane):
        self.terms, self.planes, self.my_plane = (terms, planes, my_plane)
        self.right = self.left = None
        self.steps = 0

    def part(self, place):
        return lax.dynamic_index_in_dim(
            self.terms, jnp.clip(place, 0, self.planes - 1), 0, keepdims=False
        )

    def step(self, *earlier):
        self.steps += 1
        step, planes = (self.steps, self.planes)
        right = self.part(self.my_plane + planes - step)
        left = self.part(self.my_plane - planes + step)
        if step > 1:
            right = add_rounded(self.right, right)
            left = add_rounded(self.left, left)
        if earlier:
            right = after(right, *earlier)
            left = after(left, *earlier)
        self.right = shift_planes(right, 1, range(0, step))
        self.left = shift_planes(left, -1, range(planes - step, planes))

    def last(self):
        return (self.right, self.left)

    def total(self):
        total = self.part(self.my_plane).astype(jnp.float32) + self.right.astype(jnp.float32)
        return (total + self.left.astype(jnp.float32)).astype(jnp.bfloat16)


def rows_kernel(pick_ref, count_ref, *refs):
    low_a, low_b, high_a, high_b, gain_ref = refs[:5]
    normed_ref, stats_ref = refs[-2:]
    at = pl.program_id(0)
    rows = low_a.shape[3]
    half = low_a.shape[4]
    width = 2 * half
    live = lax.broadcasted_iota(jnp.int32, (rows, 1), 0) < count_ref[at]
    near = (pick_ref[at] & 1) == 1

    def read(here, there):
        value = jnp.where(near, there[0, 0, 0], here[0, 0, 0])
        return jnp.where(live, value.astype(jnp.float32), 0.0)

    low = read(low_a, low_b)
    high = read(high_a, high_b)
    mean = (
        jnp.sum(low, axis=-1, keepdims=True) + jnp.sum(high, axis=-1, keepdims=True)
    ) / width
    low = low - mean
    high = high - mean
    variance = (
        jnp.sum(low * low, axis=-1, keepdims=True) + jnp.sum(high * high, axis=-1, keepdims=True)
    ) / width
    factor = lax.rsqrt(variance + epsilon)
    normed_ref[:, :half] = (low * factor * gain_ref[:, :half]).astype(normed_ref.dtype)
    normed_ref[:, half:] = (high * factor * gain_ref[:, half:]).astype(normed_ref.dtype)
    lane = lax.broadcasted_iota(jnp.int32, (rows, stats_ref.shape[1]), 1)
    stats_ref[...] = jnp.where(lane == 0, mean, factor)


def norm_block(here, there, picks, live_counts, norm_gain, my_group, part, parts, before):
    _, _, slots, rows, half = here.shape
    width = 2 * half
    steps = PLANE * slots
    picks = jnp.concatenate([picks, my_group[None]])

    def source(group_xor):
        return pl.BlockSpec(
            (1, 1, 1, rows, half),
            lambda at, pick, count: (pick[at] >> 1, pick[steps] ^ group_xor, at % slots, 0, 0),
        )

    out_specs = [
        pl.BlockSpec((rows, width), lambda at, pick, count: (at + part * steps, 0)),
        pl.BlockSpec((rows, 128), lambda at, pick, count: (at + part * steps, 0)),
    ]
    total = parts * steps * rows
    extra = [] if before is None else list(before)
    return pl.pallas_call(
        rows_kernel,
        grid_spec=pltpu.PrefetchScalarGridSpec(
            num_scalar_prefetch=2,
            grid=(steps,),
            in_specs=[
                source(0),
                source(0),
                source(1),
                source(1),
                pl.BlockSpec((1, width), lambda at, pick, count: (0, 0)),
            ]
            + [pl.BlockSpec(memory_space=pl.ANY)] * len(extra),
            out_specs=out_specs,
        ),
        out_shape=[
            jax.ShapeDtypeStruct((total, width), jnp.bfloat16),
            jax.ShapeDtypeStruct((total, 128), jnp.float32),
        ],
        input_output_aliases={7: 0, 8: 1} if extra else {},
        compiler_params=pltpu.CompilerParams(vmem_limit_bytes=32 * 1024 * 1024),
        cost_estimate=pl.CostEstimate(
            flops=10 * steps * rows * width,
            bytes_accessed=6 * steps * rows * width,
            transcendentals=0,
        ),
        name="norm_rows",
    )(picks, live_counts, here, there, here, there, norm_gain[None, :], *extra)


def mm(left, right, left_dim, right_dim):
    return lax.dot_general(
        left,
        right,
        (((left_dim,), (right_dim,)), ((), ())),
        preferred_element_type=jnp.float32,
    )


def attend_image(projected, grad_mixed, scales, live, rows, head_dim):
    query_hat, query_factor = norm_rows(projected[:, :head_dim])
    key_hat, key_factor = norm_rows(projected[:, head_dim : 2 * head_dim])
    query_scale = scales[0:1, :]
    key_scale = scales[1:2, :]
    query = (query_hat * query_scale).astype(jnp.bfloat16)
    key_rows = (key_hat * key_scale).astype(jnp.bfloat16)
    values = projected[:, 2 * head_dim :].astype(jnp.bfloat16)
    row_id = lax.broadcasted_iota(jnp.int32, (rows, rows), 0)
    col_id = lax.broadcasted_iota(jnp.int32, (rows, rows), 1)
    allowed = ((row_id < live) & (col_id < live)) | (row_id == col_id)
    raised = jnp.where(allowed, jnp.exp(mm(query, key_rows, 1, 1)), 0.0)
    attention = raised / jnp.sum(raised, axis=-1, keepdims=True)
    rounded = attention.astype(jnp.bfloat16)
    mixed = mm(rounded, values, 1, 0).astype(jnp.bfloat16)
    grad_value = mm(rounded, grad_mixed, 0, 0)
    grad_attention = mm(grad_mixed, values, 1, 1)
    grad_scores = attention * (
        grad_attention - jnp.sum(attention * grad_attention, axis=-1, keepdims=True)
    )
    grad_scores = grad_scores.astype(jnp.bfloat16)
    grad_query = mm(grad_scores, key_rows, 1, 0)
    grad_key = mm(grad_scores, query, 0, 0)
    query_grad = norm_back(grad_query * query_scale, query_hat, query_factor)
    key_grad = norm_back(grad_key * key_scale, key_hat, key_factor)
    return (mixed, query_grad, key_grad, grad_value)


def attention_kernel(per_step, count_ref, proj_ref, grad_ref, scale_ref, mixed_ref, back_ref):
    at = pl.program_id(0)
    rows = proj_ref.shape[0] // per_step
    head_dim = grad_ref.shape[1]
    scales = scale_ref[...]
    for image in range(per_step):
        span = slice(image * rows, (image + 1) * rows)
        mixed, query_grad, key_grad, grad_value = attend_image(
            proj_ref[span, :],
            grad_ref[span, :],
            scales,
            count_ref[at * per_step + image],
            rows,
            head_dim,
        )
        mixed_ref[span, :] = mixed
        back_ref[span, :head_dim] = query_grad.astype(jnp.bfloat16)
        back_ref[span, head_dim : 2 * head_dim] = key_grad.astype(jnp.bfloat16)
        back_ref[span, 2 * head_dim :] = grad_value.astype(jnp.bfloat16)


def attend(projected, grad_mixed, scales, live_counts, rows):
    total, head_dim = grad_mixed.shape
    image_count = total // rows
    per_step = 4
    block = per_step * rows
    return pl.pallas_call(
        functools.partial(attention_kernel, per_step),
        grid_spec=pltpu.PrefetchScalarGridSpec(
            num_scalar_prefetch=1,
            grid=(image_count // per_step,),
            in_specs=[
                pl.BlockSpec((block, 3 * head_dim), lambda at, count: (at, 0)),
                pl.BlockSpec((block, head_dim), lambda at, count: (at, 0)),
                pl.BlockSpec((2, head_dim), lambda at, count: (0, 0)),
            ],
            out_specs=[
                pl.BlockSpec((block, head_dim), lambda at, count: (at, 0)),
                pl.BlockSpec((block, 3 * head_dim), lambda at, count: (at, 0)),
            ],
        ),
        out_shape=[
            jax.ShapeDtypeStruct((total, head_dim), jnp.bfloat16),
            jax.ShapeDtypeStruct((total, 3 * head_dim), jnp.bfloat16),
        ],
        compiler_params=pltpu.CompilerParams(vmem_limit_bytes=32 * 1024 * 1024),
        cost_estimate=pl.CostEstimate(
            flops=12 * total * rows * head_dim,
            bytes_accessed=12 * total * head_dim * 2,
            transcendentals=total * rows,
        ),
        name="attend_images",
    )(live_counts, projected, grad_mixed, scales)


def scatter_partial(partial, share_width, my_group, *earlier):
    parts, _, rows, width = partial.shape

    def block(place):
        return partial[:, place].reshape(parts * rows, width)

    sent_far, sent_near = (block(3), block(1))
    if earlier:
        sent_far = after(sent_far, *earlier)
        sent_near = after(sent_near, *earlier)
    got_far = swap_fsdp(sent_far, 1)
    got_near = swap_fsdp(sent_near, 1)
    far = add_rounded(block(2), got_far)
    near = add_rounded(block(0), got_near)

    def halves(value):
        mine = lax.dynamic_slice_in_dim(value, my_group * share_width, share_width, 1)
        other = lax.dynamic_slice_in_dim(value, (1 - my_group) * share_width, share_width, 1)
        return (mine, other)

    far_mine, far_other = halves(far)
    far_got = swap_tp(far_other)
    near_mine, near_other = halves(near)
    near_got = swap_tp(after(near_other, far_got))
    far_sum = swap_fsdp(add_rounded(far_mine, far_got), 2)
    return (
        near_mine.astype(jnp.float32)
        + near_got.astype(jnp.float32)
        + far_sum.astype(jnp.float32)
    )


def per_plane(patches, cotangent, counts, masks, norm_gain, qk_gain, qkv_weight, out_weight):
    replicas = lax.axis_size("fsdp")
    groups = lax.axis_size("tp")
    planes = replicas // PLANE
    my_replica = lax.axis_index("fsdp")
    my_group = lax.axis_index("tp")
    my_plane = my_replica // PLANE
    my_place = lax.rem(my_replica, PLANE)
    tok_rows = patches.shape[0]
    images = counts.shape[1]
    slot_rows = tok_rows // images
    model_width = norm_gain.shape[0]
    share_width = model_width // groups
    head_dim = qk_gain.shape[1]
    shard_rows = qkv_weight.shape[0]
    local_heads = out_weight.shape[1] // head_dim
    heads = local_heads // PLANE
    qkv_width = 3 * head_dim
    head_width = 4 * head_dim
    parts = 2
    slots = images // parts
    part_rows = slots * slot_rows

    replica_ids = jnp.arange(replicas, dtype=jnp.int32)
    relative = jnp.arange(PLANE, dtype=jnp.int32)
    sources = (my_replica ^ relative)[:, None] ^ masks[None, :]
    live_counts = jnp.sum(
        jnp.where(replica_ids[:, None, None] == sources[None], counts[:, None, :], 0), axis=0
    ).astype(jnp.int32)
    picks = (relative[:, None] ^ (masks & (PLANE - 1))[None, :]).astype(jnp.int32)
    places = jnp.arange(slot_rows, dtype=jnp.int32)
    is_live = (places[None, :] < live_counts[0][:, None]).reshape(tok_rows)

    def by_part(table):
        return jnp.transpose(table.reshape(PLANE, parts, slots), (1, 0, 2)).reshape(parts, -1)

    part_counts = by_part(live_counts)
    part_picks = by_part(picks)
    flat_counts = part_counts.reshape(-1)

    holding = lax.dynamic_slice_in_dim(patches, my_group * share_width, share_width, 1)
    holding = holding.reshape(parts, slots, slot_rows, share_width)
    moved = [holding[part] for part in range(parts)]
    for bit_place in range(2, replicas.bit_length() - 1):
        previous = None
        for part in range(parts):
            piece = moved[part] if previous is None else after(moved[part], previous)
            partner = swap_fsdp(piece, 2**bit_place)
            moving = jnp.right_shift(masks[part * slots : (part + 1) * slots], bit_place) & 1
            moved[part] = jnp.where((moving == 1)[:, None, None], partner, moved[part])
            previous = partner

    def head_columns(place):
        qkv_part = lax.dynamic_slice_in_dim(
            qkv_weight, place * heads * qkv_width, heads * qkv_width, 1
        ).reshape(shard_rows, heads, qkv_width)
        out_part = lax.dynamic_slice_in_dim(
            out_weight, place * heads * head_dim, heads * head_dim, 1
        ).reshape(shard_rows, heads, head_dim)
        return jnp.concatenate([qkv_part, out_part], axis=2).reshape(
            shard_rows, heads * head_width
        )

    shards = [head_columns(my_place)]
    for step in range(1, PLANE):
        shards.append(swap_fsdp(head_columns(my_place ^ step), step))
    plane_shard = jnp.zeros((PLANE, shard_rows, heads * head_width), qkv_weight.dtype)
    for step in range(PLANE):
        plane_shard = lax.dynamic_update_index_in_dim(
            plane_shard, shards[step], my_place ^ step, 0
        )
    plane_shard = plane_shard.reshape(PLANE * shard_rows, heads * head_width)

    upstream_own = jnp.where(is_live[:, None], cotangent, jnp.zeros((), cotangent.dtype))
    up_own = [upstream_own[:part_rows], upstream_own[part_rows:]]
    up_near = swap_fsdp(upstream_own, 1)
    up_far = [swap_fsdp(after(up_own[0], shards[2], shards[3]), 2), None]

    here, there = ([], [])
    for part in range(parts):
        own = moved[part]
        over = swap_tp(own)
        far = swap_fsdp(own, 2)
        far_over = swap_tp(far)
        here.append(
            jnp.stack([own, over, far, far_over]).reshape(
                2, 2, slots, slot_rows, share_width
            )
        )
        there.append(swap_fsdp(here[part], 1))
    up_far[1] = swap_fsdp(after(up_own[1], far), 2)
    up_both = [swap_fsdp(value, 1) for value in up_far]
    upstream = jnp.concatenate(
        [
            value
            for part in range(parts)
            for value in (
                up_own[part],
                up_near[part * part_rows : (part + 1) * part_rows],
                up_far[part],
                up_both[part],
            )
        ]
    )

    shard_of = [
        plane_shard[:, head * head_width : (head + 1) * head_width] for head in range(heads)
    ]
    gathers = [PlaneGather(shard, planes, my_plane) for shard in shard_of]
    reduces = [None] * heads
    gathers[0].step(moved[1])
    for step in range(2, planes):
        gathers[0].step()

    normed_stats = None
    for part in range(parts):
        normed_stats = norm_block(
            here[part],
            there[part],
            part_picks[part],
            part_counts[part],
            norm_gain,
            my_group,
            part,
            parts,
            normed_stats,
        )
    normed, stats = normed_stats

    scales = jnp.concatenate([qk_gain[0:1] * head_dim ** (-0.5), qk_gain[1:2]])
    weights, mixed_parts, back_parts, grads = ([], [], [], [])
    for head in range(heads):
        weight = gathers[head].whole()
        weights.append(weight)
        if head + 1 < heads:
            gathers[head + 1].step(*gathers[head].last())
        out_head = weight[:, qkv_width:]
        grad_mixed = mm(upstream, out_head, 1, 0).astype(jnp.bfloat16)
        projected = mm(normed, weight[:, :qkv_width], 1, 0)
        if head > 0:
            projected = after(projected, *reduces[head - 1].last())
            reduces[head - 1].step()
        mixed, back = attend(projected, grad_mixed, scales, flat_counts, slot_rows)
        mixed_parts.append(mixed)
        back_parts.append(back)
        frontier = []
        if head + 1 < heads:
            frontier += gathers[head + 1].last()
        if head > 0:
            frontier += reduces[head - 1].last()
        held_back, held_mixed = (back, mixed)
        if frontier:
            held_back = after(back, *frontier)
            held_mixed = after(mixed, *frontier)
        if head + 1 < heads:
            for step in range(2, planes):
                gathers[head + 1].step(mixed)
        if head > 0:
            reduces[head - 1].step(mixed)
        qkv_term = mm(normed, held_back, 0, 0).astype(jnp.bfloat16)
        out_term = mm(upstream, held_mixed, 0, 0).astype(jnp.bfloat16)
        terms = jnp.concatenate([qkv_term, out_term], axis=1).reshape(
            planes, PLANE * shard_rows, head_width
        )
        reduces[head] = PlaneReduce(terms, planes, my_plane)
        reduces[head].step()
    while reduces[-1].steps < planes - 1:
        reduces[-1].step()

    back_all = jnp.concatenate(back_parts, axis=1)
    qkv_all = jnp.concatenate([weight[:, :qkv_width] for weight in weights], axis=1)
    partial_back = mm(back_all, qkv_all, 1, 1).astype(jnp.bfloat16)
    grad_normed = scatter_partial(
        partial_back.reshape(parts, PLANE, part_rows, model_width), share_width, my_group
    )
    mixed_all = jnp.concatenate(mixed_parts, axis=1)
    out_all = jnp.concatenate([weight[:, qkv_width:] for weight in weights], axis=1)
    partial_out = mm(mixed_all, out_all, 1, 1).astype(jnp.bfloat16)
    attended = scatter_partial(
        partial_out.reshape(parts, PLANE, part_rows, model_width), share_width, my_group
    )
    attended = jnp.where(is_live[:, None], attended, 0.0).astype(jnp.bfloat16)

    def own_slot(part, slot):
        pick = part_picks[part, slot]
        mine = lax.dynamic_index_in_dim(here[part][:, 0, slot], pick >> 1, 0, keepdims=False)
        other = lax.dynamic_index_in_dim(there[part][:, 0, slot], pick >> 1, 0, keepdims=False)
        return jnp.where((pick & 1) == 1, other, mine)

    own_rows = jnp.concatenate(
        [own_slot(part, slot) for part in range(parts) for slot in range(slots)]
    ).astype(jnp.float32)
    own_rows = jnp.where(is_live[:, None], own_rows, 0.0)
    own_stats = jnp.concatenate(
        [
            stats[part * PLANE * part_rows : part * PLANE * part_rows + part_rows, 0:2]
            for part in range(parts)
        ]
    )
    mean = own_stats[:, 0:1]
    factor = own_stats[:, 1:2]
    centred = (own_rows - mean) * factor
    gain_share = lax.dynamic_slice_in_dim(norm_gain, my_group * share_width, share_width, 0)
    weighted = grad_normed * gain_share
    sums = jnp.stack([jnp.sum(weighted, axis=-1), jnp.sum(weighted * centred, axis=-1)])
    sums = (sums + swap_tp(sums)) / model_width
    grad_rows = factor * (weighted - sums[0][:, None] - centred * sums[1][:, None])
    grad_rows = grad_rows.astype(jnp.bfloat16)

    def bring_home(sums_of):
        summed = jnp.stack(sums_of).reshape(
            len(sums_of), PLANE, shard_rows, head_width
        )
        blocks = []
        for step in range(PLANE):
            block = lax.dynamic_index_in_dim(summed, my_place ^ step, 1, keepdims=False)
            blocks.append(block if step == 0 else swap_fsdp(block, step))
        return jnp.stack(blocks)

    early = bring_home([reduce.total() for reduce in reduces[:-1]])
    late = bring_home([reduces[-1].total()])
    stacked = jnp.concatenate([early, late], axis=1)
    stacked = jnp.take(stacked, my_place ^ relative, axis=0).astype(jnp.float32)
    stacked = jnp.transpose(stacked, (2, 0, 1, 3))
    grad_qkv_weight = stacked[..., :qkv_width].reshape(shard_rows, local_heads * qkv_width)
    grad_out_weight = stacked[..., qkv_width:].reshape(shard_rows, local_heads * head_dim)
    return (attended, grad_rows, grad_qkv_weight, grad_out_weight)


def solution(mesh):
    def body(patches, cotangent, counts, masks, norm_gain, qk_gain, qkv_weight, out_weight):
        replicas = mesh.shape["fsdp"]
        local_heads = out_weight.shape[1] // qk_gain.shape[1]
        planar = (
            mesh.shape["tp"] == 2
            and replicas == 4 * PLANE
            and replicas & (replicas - 1) == 0
            and local_heads % PLANE == 0
            and qk_gain.shape[1] == 128
            and counts.shape[1] == 4
        )
        plan = per_plane if planar else per_device
        return plan(
            patches, cotangent, counts, masks, norm_gain, qk_gain, qkv_weight, out_weight
        )

    in_specs = (
        P("fsdp", None),
        P("fsdp", None),
        P(),
        P(),
        P(),
        P(),
        P("fsdp", "tp"),
        P("fsdp", "tp"),
    )
    out_specs = (P("fsdp", "tp"), P("fsdp", "tp"), P("fsdp", "tp"), P("fsdp", "tp"))
    return jax.shard_map(
        body, mesh=mesh, in_specs=in_specs, out_specs=out_specs, check_vma=False
    )
```

```python
import functools
import jax
import jax.numpy as jnp
from jax import lax
from jax.experimental import pallas as pl
from jax.experimental.pallas import tpu as pltpu
from jax.sharding import PartitionSpec as P

epsilon = 1e-06
PLANE = 4
ORDER = (1, 3, 0, 2)


def partner_2(value, axis, stride):
    mask = 2**stride
    pairs = [(source, source ^ mask) for source in range(lax.axis_size(axis))]
    return lax.ppermute(value, axis, pairs)


def norm_rows(values):
    row_mean = jnp.mean(values, axis=-1, keepdims=True)
    centred = values - row_mean
    factor = lax.rsqrt(jnp.mean(centred * centred, axis=-1, keepdims=True) + epsilon)
    return (centred * factor, factor)


def norm_back(upstream, normed, factor):
    return factor * (
        upstream
        - jnp.mean(upstream, axis=-1, keepdims=True)
        - normed * jnp.mean(upstream * normed, axis=-1, keepdims=True)
    )


def per_device(patches, cotangent, counts, masks, norm_gain, qk_gain, qkv_weight, out_weight):
    replicas = lax.axis_size("fsdp")
    groups = lax.axis_size("tp")
    my_replica = lax.axis_index("fsdp")
    my_group = lax.axis_index("tp")
    tok_rows = patches.shape[0]
    images = counts.shape[1]
    slot_rows = tok_rows // images
    model_width = norm_gain.shape[0]
    share_width = model_width // groups
    head_dim = qk_gain.shape[1]
    qkv_cols = qkv_weight.shape[1]
    out_cols = out_weight.shape[1]
    local_heads = out_cols // head_dim
    row_slot = jnp.arange(tok_rows, dtype=jnp.int32) // slot_rows
    holding = lax.dynamic_slice_in_dim(patches, my_group * share_width, share_width, 1)
    digit_count = replicas.bit_length() - 1
    digit_order = list(range(digit_count))
    for bit_place in digit_order:
        partner = partner_2(holding, "fsdp", bit_place)
        moving = jnp.bitwise_and(jnp.right_shift(masks, bit_place), 1) == 1
        take_rows = jnp.take(moving, row_slot)
        holding = jnp.where(take_rows[:, None], partner, holding)
    replica_ids = jnp.arange(replicas, dtype=jnp.int32)
    sources = jnp.bitwise_xor(my_replica, masks)
    run_counts = jnp.sum(jnp.where(replica_ids[:, None] == sources[None, :], counts, 0), axis=0)
    places = jnp.arange(slot_rows, dtype=jnp.int32)
    live_slots = places[None, :] < run_counts[:, None]
    is_live = live_slots.reshape(tok_rows)
    allowed = live_slots[:, :, None] & live_slots[:, None, :] | jnp.eye(slot_rows, dtype=bool)[None]
    packed = jnp.where(is_live[:, None], holding, jnp.zeros((), holding.dtype))
    block_rows = lax.all_gather(packed, "tp", axis=1, tiled=True)
    qkv_full, out_full = (
        lax.all_gather(qkv_weight, "fsdp", axis=0, tiled=True),
        lax.all_gather(out_weight, "fsdp", axis=0, tiled=True),
    )
    centred_rows, row_factor = norm_rows(block_rows.astype(jnp.float32))
    normed = (centred_rows * norm_gain).astype(jnp.bfloat16)
    projected = jnp.dot(normed, qkv_full, preferred_element_type=jnp.float32).reshape(
        images, slot_rows, local_heads, 3, head_dim
    )
    query_hat, query_factor = norm_rows(projected[:, :, :, 0])
    key_hat, key_factor = norm_rows(projected[:, :, :, 1])
    query_scale = qk_gain[0] * head_dim ** (-0.5)
    key_scale = qk_gain[1]
    query = (query_hat * query_scale).astype(jnp.bfloat16)
    key_rows = (key_hat * key_scale).astype(jnp.bfloat16)
    values = projected[:, :, :, 2].astype(jnp.bfloat16)
    scores = jnp.einsum("sqhe,skhe->shqk", query, key_rows, preferred_element_type=jnp.float32)
    raised = jnp.where(allowed[:, None], jnp.exp(scores), 0.0)
    attention = raised / jnp.sum(raised, axis=-1, keepdims=True)
    rounded_attention = attention.astype(jnp.bfloat16)
    mixed = jnp.einsum(
        "shqk,skhe->sqhe", rounded_attention, values, preferred_element_type=jnp.float32
    )
    mixed = mixed.astype(jnp.bfloat16).reshape(tok_rows, out_cols)
    partial_value = lax.dot_general(
        mixed, out_full, (((1,), (1,)), ((), ())), preferred_element_type=jnp.float32
    )
    attended = lax.psum_scatter(
        partial_value.astype(jnp.bfloat16), "tp", scatter_dimension=1, tiled=True
    ).astype(jnp.float32)
    attended = jnp.where(is_live[:, None], attended, 0.0).astype(jnp.bfloat16)
    upstream_rows = jnp.where(is_live[:, None], cotangent, jnp.zeros((), cotangent.dtype))
    grad_mixed = jnp.dot(upstream_rows, out_full, preferred_element_type=jnp.float32).astype(
        jnp.bfloat16
    )
    grad_heads = grad_mixed.reshape(images, slot_rows, local_heads, head_dim)
    grad_value = jnp.einsum(
        "shqk,sqhe->skhe", rounded_attention, grad_heads, preferred_element_type=jnp.float32
    )
    grad_attention = jnp.einsum(
        "sqhe,skhe->shqk", grad_heads, values, preferred_element_type=jnp.float32
    )
    grad_scores = attention * (
        grad_attention - jnp.sum(attention * grad_attention, axis=-1, keepdims=True)
    )
    grad_scores = grad_scores.astype(jnp.bfloat16)
    grad_query = jnp.einsum(
        "shqk,skhe->sqhe", grad_scores, key_rows, preferred_element_type=jnp.float32
    )
    grad_key = jnp.einsum("shqk,sqhe->skhe", grad_scores, query, preferred_element_type=jnp.float32)
    query_grad = norm_back(grad_query * query_scale, query_hat, query_factor)
    key_grad = norm_back(grad_key * key_scale, key_hat, key_factor)
    grad_qkv = (
        jnp.stack([query_grad, key_grad, grad_value], axis=3)
        .astype(jnp.bfloat16)
        .reshape(tok_rows, qkv_cols)
    )
    qkv_term = lax.dot_general(
        normed, grad_qkv, (((0,), (0,)), ((), ())), preferred_element_type=jnp.float32
    )
    out_term = lax.dot_general(
        upstream_rows, mixed, (((0,), (0,)), ((), ())), preferred_element_type=jnp.float32
    )
    stacked = lax.psum_scatter(
        jnp.concatenate([qkv_term, out_term], axis=1).astype(jnp.bfloat16),
        "fsdp",
        scatter_dimension=0,
        tiled=True,
    ).astype(jnp.float32)
    grad_qkv_weight = stacked[:, :qkv_cols]
    grad_out_weight = stacked[:, qkv_cols:]
    partial_back = lax.dot_general(
        grad_qkv, qkv_full, (((1,), (1,)), ((), ())), preferred_element_type=jnp.float32
    )
    summed = lax.psum(partial_back.astype(jnp.bfloat16), "tp").astype(jnp.float32)
    grad_full = norm_back(summed * norm_gain, centred_rows, row_factor)
    grad_share = lax.dynamic_slice_in_dim(grad_full, my_group * share_width, share_width, 1)
    grad_rows = grad_share.astype(jnp.bfloat16)
    return (attended, grad_rows, grad_qkv_weight, grad_out_weight)


def swap_fsdp(value, mask):
    pairs = [(source, source ^ mask) for source in range(lax.axis_size("fsdp"))]
    return lax.ppermute(value, "fsdp", pairs)


def swap_tp(value):
    return lax.ppermute(value, "tp", [(0, 1), (1, 0)])


def send_planes(value, plane_pairs):
    pairs = [
        (source * PLANE + place, target * PLANE + place)
        for source, target in plane_pairs
        for place in range(PLANE)
    ]
    return lax.ppermute(value, "fsdp", pairs)


def after(value, *earlier):
    return lax.optimization_barrier((value,) + earlier)[0]


def spread_places(blocks):
    near = swap_fsdp(jnp.stack([blocks[1], blocks[3]]), 1)
    far = swap_fsdp(jnp.stack([blocks[2], near[1]]), 2)
    return [blocks[0], near[0], far[0], far[1]]


class LineGather:
    def __init__(self, own, my_plane):
        self.own, self.my_plane = (own, my_plane)

    def pair_up(self, *earlier):
        self.partner = swap_fsdp(after(self.own, *earlier), PLANE)

    def cross(self, *earlier):
        even = self.my_plane % 2 == 0
        partner = after(self.partner, *earlier)
        low = jnp.where(even, self.own, partner)
        high = jnp.where(even, partner, self.own)
        self.pair = jnp.concatenate([low, high])
        self.crossed = send_planes(self.pair, [(1, 2), (2, 1)])

    def spread(self, *earlier):
        self.outer = send_planes(after(self.crossed, *earlier), [(1, 0), (2, 3)])

    def whole(self, *earlier):
        inner = (self.my_plane == 1) | (self.my_plane == 2)
        crossed, outer = lax.optimization_barrier((self.crossed, self.outer) + earlier)[:2]
        other = jnp.where(inner, crossed, outer)
        low = self.my_plane < 2
        return jnp.concatenate([jnp.where(low, self.pair, other), jnp.where(low, other, self.pair)])


def pair_up_both(first, second, *earlier):
    both = after(jnp.stack([first.own, second.own]), *earlier)
    both = swap_fsdp(both, PLANE)
    first.partner, second.partner = (both[0], both[1])


def add_rounded(left, right):
    return (left.astype(jnp.float32) + right.astype(jnp.float32)).astype(jnp.bfloat16)


class LineReduce:
    def __init__(self, terms, my_plane):
        self.terms, self.my_plane = (terms, my_plane)
        self.rows = terms[0].shape[1] // 4
        self.far = 2 - 2 * (my_plane // 2)

    def columns(self, start, count):
        return jnp.concatenate(
            [
                lax.dynamic_slice_in_dim(term, start * self.rows, count * self.rows, 1)
                for term in self.terms
            ]
        )

    def inward(self):
        self.sent = self.columns(self.far, 2)
        self.arrived = send_planes(self.sent, [(0, 1), (3, 2)])

    def cross(self, *earlier):
        far = add_rounded(self.columns(self.far, 2), after(self.arrived, *earlier))
        self.cross_sent = far
        self.crossed = send_planes(far, [(1, 2), (2, 1)])

    def of_pair(self, plane, *earlier):
        crossed = after(self.crossed, *earlier)
        crossed = lax.dynamic_slice_in_dim(crossed, plane % 2 * self.rows, self.rows, 1)
        return self.columns(plane, 1).astype(jnp.float32) + crossed.astype(jnp.float32)


def reduce_pairs(reduces, my_plane, *earlier):
    sent = jnp.concatenate([reduce.of_pair(my_plane ^ 1, *earlier) for reduce in reduces])
    sent = sent.astype(jnp.bfloat16)
    got = swap_fsdp(sent, PLANE)

    def total(*later):
        kept = jnp.concatenate([reduce.of_pair(my_plane, *later) for reduce in reduces])
        return (kept + after(got, *later).astype(jnp.float32)).astype(jnp.bfloat16)

    return (sent, total)


def rows_kernel(parts, pick_ref, count_ref, *refs):
    sources, (gain_ref, normed_ref, stats_ref) = (refs[:-3], refs[-3:])
    at = pl.program_id(0)
    rows, half = sources[0].shape[3:]
    width = 2 * half
    live = lax.broadcasted_iota(jnp.int32, (rows, 1), 0) < count_ref[at]
    near = (pick_ref[at] & 1) == 1
    part = at // (pl.num_programs(0) // parts)

    def read(high):
        value = None
        for index in range(parts):
            here, there = sources[4 * index + high], sources[4 * index + 2 + high]
            chosen = jnp.where(near, there[0, 0, 0], here[0, 0, 0])
            value = chosen if value is None else jnp.where(part == index, chosen, value)
        return jnp.where(live, value.astype(jnp.float32), 0.0)

    low = read(0)
    high = read(1)
    mean = (
        jnp.sum(low, axis=-1, keepdims=True) + jnp.sum(high, axis=-1, keepdims=True)
    ) / width
    low = low - mean
    high = high - mean
    variance = (
        jnp.sum(low * low, axis=-1, keepdims=True) + jnp.sum(high * high, axis=-1, keepdims=True)
    ) / width
    factor = lax.rsqrt(variance + epsilon)
    normed_ref[:, :half] = (low * factor * gain_ref[:, :half]).astype(normed_ref.dtype)
    normed_ref[:, half:] = (high * factor * gain_ref[:, half:]).astype(normed_ref.dtype)
    lane = lax.broadcasted_iota(jnp.int32, (rows, stats_ref.shape[1]), 1)
    stats_ref[...] = jnp.where(lane == 0, mean, factor)


def norm_block(here, there, picks, live_counts, norm_gain, my_group):
    parts = len(here)
    _, _, slots, rows, half = here[0].shape
    width = 2 * half
    steps = PLANE * slots
    total = parts * steps
    picks = jnp.concatenate([picks, my_group[None]])

    def source(part, group_xor, near):
        def index(at, pick, count):
            at = jnp.clip(at, part * steps, part * steps + steps - 1)
            first = at // PLANE * PLANE
            stand_in = jnp.where(at - first < 2, first + 2, first + 1)
            chosen = pick[jnp.where((pick[at] & 1) == near, at, stand_in)]
            return (chosen >> 1, pick[total] ^ group_xor, at // PLANE % slots, 0, 0)

        return pl.BlockSpec((1, 1, 1, rows, half), index)

    def target(at, pick, count):
        slot, place = (at // PLANE, at % PLANE)
        return (place * parts * slots + slot, 0)

    arrays, specs = ([], [])
    for part in range(parts):
        arrays += [here[part], here[part], there[part], there[part]]
        specs += [source(part, 0, 0), source(part, 1, 0), source(part, 0, 1), source(part, 1, 1)]
    return pl.pallas_call(
        functools.partial(rows_kernel, parts),
        grid_spec=pltpu.PrefetchScalarGridSpec(
            num_scalar_prefetch=2,
            grid=(total,),
            in_specs=specs + [pl.BlockSpec((1, width), lambda at, pick, count: (0, 0))],
            out_specs=[pl.BlockSpec((rows, width), target), pl.BlockSpec((rows, 128), target)],
        ),
        out_shape=[
            jax.ShapeDtypeStruct((total * rows, width), jnp.bfloat16),
            jax.ShapeDtypeStruct((total * rows, 128), jnp.float32),
        ],
        compiler_params=pltpu.CompilerParams(vmem_limit_bytes=28 * 1024 * 1024),
        cost_estimate=pl.CostEstimate(
            flops=10 * total * rows * width,
            bytes_accessed=6 * total * rows * width,
            transcendentals=0,
        ),
        name="norm_rows",
    )(picks, live_counts, *arrays, norm_gain[None, :])


def mm(left, right, left_dim, right_dim):
    return lax.dot_general(
        left,
        right,
        (((left_dim,), (right_dim,)), ((), ())),
        preferred_element_type=jnp.float32,
    )


def attend_image(projected, grad_mixed, scales, live, rows, head_dim):
    query_hat, query_factor = norm_rows(projected[:, :head_dim])
    key_hat, key_factor = norm_rows(projected[:, head_dim : 2 * head_dim])
    query_scale = scales[0:1, :]
    key_scale = scales[1:2, :]
    query = (query_hat * query_scale).astype(jnp.bfloat16)
    key_rows = (key_hat * key_scale).astype(jnp.bfloat16)
    values = projected[:, 2 * head_dim :].astype(jnp.bfloat16)
    row_id = lax.broadcasted_iota(jnp.int32, (rows, rows), 0)
    col_id = lax.broadcasted_iota(jnp.int32, (rows, rows), 1)
    allowed = ((row_id < live) & (col_id < live)) | (row_id == col_id)
    raised = jnp.where(allowed, jnp.exp(mm(query, key_rows, 1, 1)), 0.0)
    attention = raised / jnp.sum(raised, axis=-1, keepdims=True)
    rounded = attention.astype(jnp.bfloat16)
    mixed = mm(rounded, values, 1, 0).astype(jnp.bfloat16)
    grad_value = mm(rounded, grad_mixed, 0, 0)
    grad_attention = mm(grad_mixed, values, 1, 1)
    grad_scores = attention * (
        grad_attention - jnp.sum(attention * grad_attention, axis=-1, keepdims=True)
    )
    grad_scores = grad_scores.astype(jnp.bfloat16)
    grad_query = mm(grad_scores, key_rows, 1, 0)
    grad_key = mm(grad_scores, query, 0, 0)
    query_grad = norm_back(grad_query * query_scale, query_hat, query_factor)
    key_grad = norm_back(grad_key * key_scale, key_hat, key_factor)
    return (mixed, query_grad, key_grad, grad_value)


def attention_kernel(per_step, count_ref, proj_ref, grad_ref, scale_ref, mixed_ref, back_ref):
    at = pl.program_id(0)
    rows = proj_ref.shape[0] // per_step
    head_dim = grad_ref.shape[1]
    scales = scale_ref[...]
    for image in range(per_step):
        span = slice(image * rows, (image + 1) * rows)
        mixed, query_grad, key_grad, grad_value = attend_image(
            proj_ref[span, :],
            grad_ref[span, :],
            scales,
            count_ref[at * per_step + image],
            rows,
            head_dim,
        )
        mixed_ref[span, :] = mixed
        back_ref[span, :head_dim] = query_grad.astype(jnp.bfloat16)
        back_ref[span, head_dim : 2 * head_dim] = key_grad.astype(jnp.bfloat16)
        back_ref[span, 2 * head_dim :] = grad_value.astype(jnp.bfloat16)


def attend(projected, grad_mixed, scales, live_counts, rows):
    total, head_dim = grad_mixed.shape
    image_count = total // rows
    per_step = 4
    block = per_step * rows
    return pl.pallas_call(
        functools.partial(attention_kernel, per_step),
        grid_spec=pltpu.PrefetchScalarGridSpec(
            num_scalar_prefetch=1,
            grid=(image_count // per_step,),
            in_specs=[
                pl.BlockSpec((block, 3 * head_dim), lambda at, count: (at, 0)),
                pl.BlockSpec((block, head_dim), lambda at, count: (at, 0)),
                pl.BlockSpec((2, head_dim), lambda at, count: (0, 0)),
            ],
            out_specs=[
                pl.BlockSpec((block, head_dim), lambda at, count: (at, 0)),
                pl.BlockSpec((block, 3 * head_dim), lambda at, count: (at, 0)),
            ],
        ),
        out_shape=[
            jax.ShapeDtypeStruct((total, head_dim), jnp.bfloat16),
            jax.ShapeDtypeStruct((total, 3 * head_dim), jnp.bfloat16),
        ],
        compiler_params=pltpu.CompilerParams(vmem_limit_bytes=32 * 1024 * 1024),
        cost_estimate=pl.CostEstimate(
            flops=12 * total * rows * head_dim,
            bytes_accessed=12 * total * head_dim * 2,
            transcendentals=total * rows,
        ),
        name="attend_images",
    )(live_counts, projected, grad_mixed, scales)


class PlaneScatter:
    def __init__(self, sent, share_width, my_group):
        self.share_width, self.my_group = (share_width, my_group)
        self.got = swap_fsdp(sent, 1)

    def mine(self, value):
        start = self.my_group * self.share_width
        return lax.dynamic_slice_in_dim(value, start, self.share_width, value.ndim - 1)

    def other(self, value):
        start = (1 - self.my_group) * self.share_width
        return lax.dynamic_slice_in_dim(value, start, self.share_width, value.ndim - 1)

    def add_cores(self, kept, *earlier):
        got = after(self.got, *earlier) if earlier else self.got
        half = kept.shape[1] // 2
        first = add_rounded(kept[:, :half], got[:, :half])
        near = add_rounded(kept[0, half:], got[0, half:])
        far = add_rounded(kept[1, half:], got[1, half:])
        self.first, self.near = (first, near)
        sent_x = self.other(first)
        self.over_x = swap_tp(sent_x)
        self.over_y = swap_fsdp(far, 2)
        return (first, far, sent_x)

    def turn(self, *earlier):
        over_x = after(self.over_x, *earlier)
        over_y = after(self.over_y, *earlier)
        first = self.mine(self.first).astype(jnp.float32) + over_x.astype(jnp.float32)
        second = self.near.astype(jnp.float32) + over_y.astype(jnp.float32)
        self.first_sum = first[0]
        self.second_sum = self.mine(second)
        sent_y = first[1].astype(jnp.bfloat16)
        sent_x = self.other(second).astype(jnp.bfloat16)
        self.last_y = swap_fsdp(sent_y, 2)
        self.last_x = swap_tp(sent_x)
        return (sent_y, sent_x)

    def total(self):
        return jnp.concatenate(
            [
                self.first_sum + self.last_y.astype(jnp.float32),
                self.second_sum + self.last_x.astype(jnp.float32),
            ]
        )


def home_kernel(counts, place_ref, *refs):
    qkv_ref, out_ref = refs[-2:]
    at, head = (pl.program_id(0), pl.program_id(1))
    width = qkv_ref.shape[1]
    first = 0
    for group, count in enumerate(counts):
        inside = (head >= first) & (head < first + count)
        for step in range(PLANE):

            @pl.when((at == step) & inside)
            def _():
                value = refs[group * PLANE + step][...].astype(jnp.float32)
                qkv_ref[...] = value[:, :width]
                out_ref[...] = value[:, width:]

        first += count


def place_home(groups, my_place, heads, head_dim):
    rows = groups[0][0].shape[0]
    head_width = 4 * head_dim
    qkv_width = 3 * head_dim
    counts = [blocks[0].shape[1] // head_width for blocks in groups]

    def source(first, count):
        return pl.BlockSpec(
            (rows, head_width), lambda at, head, place: (0, jnp.clip(head - first, 0, count - 1))
        )

    specs = []
    for group, count in enumerate(counts):
        specs += [source(sum(counts[:group]), count)] * PLANE

    def target(at, head, place):
        return (0, (place[0] ^ at) * heads + head)

    total = PLANE * heads
    return pl.pallas_call(
        functools.partial(home_kernel, counts),
        grid_spec=pltpu.PrefetchScalarGridSpec(
            num_scalar_prefetch=1,
            grid=(PLANE, heads),
            in_specs=specs,
            out_specs=[
                pl.BlockSpec((rows, qkv_width), target),
                pl.BlockSpec((rows, head_dim), target),
            ],
        ),
        out_shape=[
            jax.ShapeDtypeStruct((rows, total * qkv_width), jnp.float32),
            jax.ShapeDtypeStruct((rows, total * head_dim), jnp.float32),
        ],
        compiler_params=pltpu.CompilerParams(vmem_limit_bytes=32 * 1024 * 1024),
        cost_estimate=pl.CostEstimate(
            flops=total * rows * head_width,
            bytes_accessed=6 * total * rows * head_width,
            transcendentals=0,
        ),
        name="place_home",
    )(my_place[None], *[block for blocks in groups for block in blocks])


def per_plane(patches, cotangent, counts, masks, norm_gain, qk_gain, qkv_weight, out_weight):
    replicas = lax.axis_size("fsdp")
    groups = lax.axis_size("tp")
    planes = replicas // PLANE
    my_replica = lax.axis_index("fsdp")
    my_group = lax.axis_index("tp")
    my_plane = my_replica // PLANE
    my_place = lax.rem(my_replica, PLANE)
    tok_rows = patches.shape[0]
    images = counts.shape[1]
    slot_rows = tok_rows // images
    model_width = norm_gain.shape[0]
    share_width = model_width // groups
    head_dim = qk_gain.shape[1]
    shard_rows = qkv_weight.shape[0]
    local_heads = out_weight.shape[1] // head_dim
    heads = local_heads // PLANE
    qkv_width = 3 * head_dim
    head_width = 4 * head_dim
    parts = 2
    slots = images // parts
    part_rows = slots * slot_rows

    replica_ids = jnp.arange(replicas, dtype=jnp.int32)
    relative = jnp.array(ORDER, dtype=jnp.int32)
    own_at = ORDER.index(0)
    sources = (my_replica ^ relative)[:, None] ^ masks[None, :]
    live_counts = jnp.sum(
        jnp.where(replica_ids[:, None, None] == sources[None], counts[:, None, :], 0), axis=0
    ).astype(jnp.int32)
    picks = (relative[:, None] ^ (masks & (PLANE - 1))[None, :]).astype(jnp.int32)
    places = jnp.arange(slot_rows, dtype=jnp.int32)
    is_live = (places[None, :] < live_counts[own_at][:, None]).reshape(tok_rows)

    def by_part(table):
        return jnp.transpose(table).reshape(-1)

    flat_counts = live_counts.reshape(-1)

    holding = lax.dynamic_slice_in_dim(patches, my_group * share_width, share_width, 1)
    holding = holding.reshape(parts, slots, slot_rows, share_width)
    moved = [holding[part] for part in range(parts)]
    first_moved = None
    for bit_place in range(2, replicas.bit_length() - 1):
        previous = None
        for part in range(parts):
            piece = moved[part] if previous is None else after(moved[part], previous)
            partner = swap_fsdp(piece, 2**bit_place)
            moving = jnp.right_shift(masks[part * slots : (part + 1) * slots], bit_place) & 1
            moved[part] = jnp.where((moving == 1)[:, None, None], partner, moved[part])
            previous = partner
            if first_moved is None:
                first_moved = moved[0]
            if part == 0:
                first_there = partner
            if part == 1 and bit_place == 2:
                second_moved = moved[1]

    def head_columns(place):
        qkv_part = lax.dynamic_slice_in_dim(
            qkv_weight, place * heads * qkv_width, heads * qkv_width, 1
        )
        out_part = lax.dynamic_slice_in_dim(
            out_weight, place * heads * head_dim, heads * head_dim, 1
        )
        return jnp.concatenate([qkv_part, out_part], axis=1)

    upstream_own = jnp.where(is_live[:, None], cotangent, jnp.zeros((), cotangent.dtype))
    up_far = [swap_fsdp(upstream_own[:part_rows], 2)]
    shards = spread_places([head_columns(my_place ^ step) for step in range(PLANE)])
    shards = [after(shard, first_moved, up_far[0]) for shard in shards]
    plane_shard = jnp.zeros((PLANE, shard_rows, heads * head_width), qkv_weight.dtype)
    for step in range(PLANE):
        plane_shard = lax.dynamic_update_index_in_dim(
            plane_shard, shards[step], my_place ^ step, 0
        )
    plane_shard = plane_shard.reshape(PLANE * shard_rows, heads * head_width)
    shards_of = []
    for head in range(heads):
        qkv_at = head * qkv_width
        out_at = heads * qkv_width + head * head_dim
        shard = jnp.concatenate(
            [
                plane_shard[:, qkv_at : qkv_at + qkv_width],
                plane_shard[:, out_at : out_at + head_dim],
            ],
            axis=1,
        )
        shards_of.append(shard)

    gathers = [LineGather(shard, my_plane) for shard in shards_of]
    gathers[0].pair_up(first_there)
    gathers[0].cross(moved[-1])

    here, there = ([], [])
    for part in range(parts):
        own = moved[part]
        over = swap_tp(own)
        if part == 0:
            far = swap_fsdp(after(own, second_moved, *shards), 2)
            far_over = swap_tp(far)
        else:
            far = swap_fsdp(after(own, gathers[0].partner), 2)
            far_over = swap_tp(after(far, over, here[0]))
            pair_up_both(gathers[1], gathers[2], gathers[0].partner)
            up_far.append(swap_fsdp(after(upstream_own[part_rows:], far), 2))
            own = after(own, gathers[0].crossed, gathers[1].partner)
        here.append(
            jnp.stack([own, over, far, far_over]).reshape(
                2, 2, slots, slot_rows, share_width
            )
        )
        there.append(swap_fsdp(here[part], 1))
    gathers[0].spread()
    gathers[1].cross()

    normed, stats = norm_block(
        here,
        there,
        by_part(picks),
        by_part(live_counts),
        norm_gain,
        my_group,
    )
    gathers[1].spread(normed)
    gathers[2].cross(normed)
    up_far[1] = after(up_far[1], normed)
    up_other = [
        swap_fsdp(jnp.stack([upstream_own[:part_rows], up_far[0]]), 1),
        swap_fsdp(jnp.stack([upstream_own[part_rows:], up_far[1]]), 1),
    ]
    upstream = jnp.concatenate(
        [up_other[0][0], up_other[1][0], up_other[0][1], up_other[1][1], upstream_own, *up_far]
    )

    scales = jnp.concatenate([qk_gain[0:1] * head_dim ** (-0.5), qk_gain[1:2]])
    weights, mixed_parts, back_parts, reduces = ([], [], [], [])
    for head in range(heads):
        if head == 0:
            weight = gathers[0].whole(normed, gathers[1].crossed, gathers[2].partner)
        elif head == 1:
            weight = gathers[1].whole(qkv_term, out_term, gathers[2].crossed)
            gathers[2].spread(qkv_term)
        else:
            weight = gathers[2].whole(qkv_term, out_term, reduces[0].cross_sent)
        weights.append(weight)
        grad_mixed = mm(upstream, weight[:, qkv_width:], 1, 0).astype(jnp.bfloat16)
        projected = mm(normed, weight[:, :qkv_width], 1, 0)
        mixed, back = attend(projected, grad_mixed, scales, flat_counts, slot_rows)
        mixed_parts.append(mixed)
        back_parts.append(back)
        held_back, held_mixed = (back, mixed)
        if head == 2:
            mixed_all = after(jnp.concatenate(mixed_parts, axis=1), reduces[1].arrived)
            out_all = jnp.concatenate([weight[:, qkv_width:] for weight in weights], axis=1)
            out_sent = mm(mixed_all[: 2 * tok_rows], out_all, 1, 1).astype(jnp.bfloat16)
            out_scatter = PlaneScatter(
                out_sent.reshape(2, tok_rows, model_width), share_width, my_group
            )
            reduces[1].cross(out_sent)
            held = after(mixed_all[2 * tok_rows :], out_sent, reduces[1].cross_sent)
            out_kept = mm(held, out_all, 1, 1).astype(jnp.bfloat16)
            held_back = after(held_back, out_kept)
            held_mixed = after(held_mixed, out_kept)
        qkv_term = mm(held_back, normed, 0, 0).astype(jnp.bfloat16)
        out_term = mm(held_mixed, upstream, 0, 0).astype(jnp.bfloat16)
        if head == 1:
            reduces[0].cross(qkv_term, out_term)
        reduces.append(LineReduce([qkv_term, out_term], my_plane))
        reduces[head].inward()

    def send_home(total):
        count = total.shape[0] // head_width
        summed = total.T.reshape(PLANE, shard_rows, count * head_width)
        return spread_places(
            [
                lax.dynamic_index_in_dim(summed, my_place ^ step, 0, keepdims=False)
                for step in range(PLANE)
            ]
        )

    back_all = jnp.concatenate(back_parts, axis=1)
    qkv_all = jnp.concatenate([weight[:, :qkv_width] for weight in weights], axis=1)
    out_added = out_scatter.add_cores(
        after(out_kept.reshape(2, tok_rows, model_width), qkv_term, out_term)
    )
    held = after(back_all[: 2 * tok_rows], *out_added, reduces[2].sent)
    back_sent = mm(held, qkv_all, 1, 1).astype(jnp.bfloat16)
    reduces[2].cross(back_sent)
    sent, early_total = reduce_pairs(reduces[:2], my_plane, back_sent)
    between = (reduces[2].cross_sent, sent)
    back_scatter = PlaneScatter(
        after(
            back_sent.reshape(2, tok_rows, model_width),
            out_scatter.over_x,
            out_scatter.over_y,
            *between,
        ),
        share_width,
        my_group,
    )
    turned = out_scatter.turn(*between)
    held = after(back_all[2 * tok_rows :], *turned)
    back_kept = mm(held, qkv_all, 1, 1).astype(jnp.bfloat16)
    back_added = back_scatter.add_cores(
        after(
            back_kept.reshape(2, tok_rows, model_width), out_scatter.last_x, out_scatter.last_y
        )
    )
    sent, late_total = reduce_pairs(reduces[2:], my_plane, *back_added)
    total = jnp.concatenate([early_total(*back_added), late_total(*back_added)])
    back_scatter.turn(sent)
    home = send_home(after(total, back_scatter.over_x, back_scatter.over_y))
    attended = out_scatter.total()
    attended = jnp.where(is_live[:, None], attended, 0.0).astype(jnp.bfloat16)
    grad_normed = back_scatter.total()

    def own_slot(part, slot):
        pick = picks[own_at, part * slots + slot]
        mine = lax.dynamic_index_in_dim(here[part][:, 0, slot], pick >> 1, 0, keepdims=False)
        other = lax.dynamic_index_in_dim(there[part][:, 0, slot], pick >> 1, 0, keepdims=False)
        return jnp.where((pick & 1) == 1, other, mine)

    own_rows = jnp.concatenate(
        [own_slot(part, slot) for part in range(parts) for slot in range(slots)]
    ).astype(jnp.float32)
    own_rows = jnp.where(is_live[:, None], own_rows, 0.0)
    own_stats = stats[own_at * tok_rows : (own_at + 1) * tok_rows, 0:2]
    mean = own_stats[:, 0:1]
    factor = own_stats[:, 1:2]
    centred = (own_rows - mean) * factor
    gain_share = lax.dynamic_slice_in_dim(norm_gain, my_group * share_width, share_width, 0)
    weighted = grad_normed * gain_share
    sums = jnp.stack([jnp.sum(weighted, axis=-1), jnp.sum(weighted * centred, axis=-1)])
    sums = (sums + swap_tp(sums)) / model_width
    grad_rows = factor * (weighted - sums[0][:, None] - centred * sums[1][:, None])
    grad_rows = grad_rows.astype(jnp.bfloat16)

    grad_qkv_weight, grad_out_weight = place_home([home], my_place, heads, head_dim)
    return (attended, grad_rows, grad_qkv_weight, grad_out_weight)


def solution(mesh):
    def body(patches, cotangent, counts, masks, norm_gain, qk_gain, qkv_weight, out_weight):
        replicas = mesh.shape["fsdp"]
        local_heads = out_weight.shape[1] // qk_gain.shape[1]
        planar = (
            mesh.shape["tp"] == 2
            and replicas == 4 * PLANE
            and replicas & (replicas - 1) == 0
            and local_heads == 3 * PLANE
            and qk_gain.shape[1] == 128
            and counts.shape[1] == 4
        )
        plan = per_plane if planar else per_device
        return plan(
            patches, cotangent, counts, masks, norm_gain, qk_gain, qkv_weight, out_weight
        )

    in_specs = (
        P("fsdp", None),
        P("fsdp", None),
        P(),
        P(),
        P(),
        P(),
        P("fsdp", "tp"),
        P("fsdp", "tp"),
    )
    out_specs = (P("fsdp", "tp"), P("fsdp", "tp"), P("fsdp", "tp"), P("fsdp", "tp"))
    return jax.shard_map(
        body, mesh=mesh, in_specs=in_specs, out_specs=out_specs, check_vma=False
    )
```

```python
import functools
import jax
import jax.numpy as jnp
from jax import lax
from jax.experimental import pallas as pl
from jax.experimental.pallas import tpu as pltpu
from jax.sharding import PartitionSpec as P

epsilon = 1e-06
PLANE = 4
ORDER = (1, 3, 0, 2)


def partner_2(value, axis, stride):
    mask = 2**stride
    pairs = [(source, source ^ mask) for source in range(lax.axis_size(axis))]
    return lax.ppermute(value, axis, pairs)


def norm_rows(values):
    row_mean = jnp.mean(values, axis=-1, keepdims=True)
    centred = values - row_mean
    factor = lax.rsqrt(jnp.mean(centred * centred, axis=-1, keepdims=True) + epsilon)
    return (centred * factor, factor)


def norm_back(upstream, normed, factor):
    return factor * (
        upstream
        - jnp.mean(upstream, axis=-1, keepdims=True)
        - normed * jnp.mean(upstream * normed, axis=-1, keepdims=True)
    )


def per_device(patches, cotangent, counts, masks, norm_gain, qk_gain, qkv_weight, out_weight):
    replicas = lax.axis_size("fsdp")
    groups = lax.axis_size("tp")
    my_replica = lax.axis_index("fsdp")
    my_group = lax.axis_index("tp")
    tok_rows = patches.shape[0]
    images = counts.shape[1]
    slot_rows = tok_rows // images
    model_width = norm_gain.shape[0]
    share_width = model_width // groups
    head_dim = qk_gain.shape[1]
    qkv_cols = qkv_weight.shape[1]
    out_cols = out_weight.shape[1]
    local_heads = out_cols // head_dim
    row_slot = jnp.arange(tok_rows, dtype=jnp.int32) // slot_rows
    holding = lax.dynamic_slice_in_dim(patches, my_group * share_width, share_width, 1)
    digit_count = replicas.bit_length() - 1
    digit_order = list(range(digit_count))
    for bit_place in digit_order:
        partner = partner_2(holding, "fsdp", bit_place)
        moving = jnp.bitwise_and(jnp.right_shift(masks, bit_place), 1) == 1
        take_rows = jnp.take(moving, row_slot)
        holding = jnp.where(take_rows[:, None], partner, holding)
    replica_ids = jnp.arange(replicas, dtype=jnp.int32)
    sources = jnp.bitwise_xor(my_replica, masks)
    run_counts = jnp.sum(jnp.where(replica_ids[:, None] == sources[None, :], counts, 0), axis=0)
    places = jnp.arange(slot_rows, dtype=jnp.int32)
    live_slots = places[None, :] < run_counts[:, None]
    is_live = live_slots.reshape(tok_rows)
    allowed = live_slots[:, :, None] & live_slots[:, None, :] | jnp.eye(slot_rows, dtype=bool)[None]
    packed = jnp.where(is_live[:, None], holding, jnp.zeros((), holding.dtype))
    block_rows = lax.all_gather(packed, "tp", axis=1, tiled=True)
    qkv_full, out_full = (
        lax.all_gather(qkv_weight, "fsdp", axis=0, tiled=True),
        lax.all_gather(out_weight, "fsdp", axis=0, tiled=True),
    )
    centred_rows, row_factor = norm_rows(block_rows.astype(jnp.float32))
    normed = (centred_rows * norm_gain).astype(jnp.bfloat16)
    projected = jnp.dot(normed, qkv_full, preferred_element_type=jnp.float32).reshape(
        images, slot_rows, local_heads, 3, head_dim
    )
    query_hat, query_factor = norm_rows(projected[:, :, :, 0])
    key_hat, key_factor = norm_rows(projected[:, :, :, 1])
    query_scale = qk_gain[0] * head_dim ** (-0.5)
    key_scale = qk_gain[1]
    query = (query_hat * query_scale).astype(jnp.bfloat16)
    key_rows = (key_hat * key_scale).astype(jnp.bfloat16)
    values = projected[:, :, :, 2].astype(jnp.bfloat16)
    scores = jnp.einsum("sqhe,skhe->shqk", query, key_rows, preferred_element_type=jnp.float32)
    raised = jnp.where(allowed[:, None], jnp.exp(scores), 0.0)
    attention = raised / jnp.sum(raised, axis=-1, keepdims=True)
    rounded_attention = attention.astype(jnp.bfloat16)
    mixed = jnp.einsum(
        "shqk,skhe->sqhe", rounded_attention, values, preferred_element_type=jnp.float32
    )
    mixed = mixed.astype(jnp.bfloat16).reshape(tok_rows, out_cols)
    partial_value = lax.dot_general(
        mixed, out_full, (((1,), (1,)), ((), ())), preferred_element_type=jnp.float32
    )
    attended = lax.psum_scatter(
        partial_value.astype(jnp.bfloat16), "tp", scatter_dimension=1, tiled=True
    ).astype(jnp.float32)
    attended = jnp.where(is_live[:, None], attended, 0.0).astype(jnp.bfloat16)
    upstream_rows = jnp.where(is_live[:, None], cotangent, jnp.zeros((), cotangent.dtype))
    grad_mixed = jnp.dot(upstream_rows, out_full, preferred_element_type=jnp.float32).astype(
        jnp.bfloat16
    )
    grad_heads = grad_mixed.reshape(images, slot_rows, local_heads, head_dim)
    grad_value = jnp.einsum(
        "shqk,sqhe->skhe", rounded_attention, grad_heads, preferred_element_type=jnp.float32
    )
    grad_attention = jnp.einsum(
        "sqhe,skhe->shqk", grad_heads, values, preferred_element_type=jnp.float32
    )
    grad_scores = attention * (
        grad_attention - jnp.sum(attention * grad_attention, axis=-1, keepdims=True)
    )
    grad_scores = grad_scores.astype(jnp.bfloat16)
    grad_query = jnp.einsum(
        "shqk,skhe->sqhe", grad_scores, key_rows, preferred_element_type=jnp.float32
    )
    grad_key = jnp.einsum("shqk,sqhe->skhe", grad_scores, query, preferred_element_type=jnp.float32)
    query_grad = norm_back(grad_query * query_scale, query_hat, query_factor)
    key_grad = norm_back(grad_key * key_scale, key_hat, key_factor)
    grad_qkv = (
        jnp.stack([query_grad, key_grad, grad_value], axis=3)
        .astype(jnp.bfloat16)
        .reshape(tok_rows, qkv_cols)
    )
    qkv_term = lax.dot_general(
        normed, grad_qkv, (((0,), (0,)), ((), ())), preferred_element_type=jnp.float32
    )
    out_term = lax.dot_general(
        upstream_rows, mixed, (((0,), (0,)), ((), ())), preferred_element_type=jnp.float32
    )
    stacked = lax.psum_scatter(
        jnp.concatenate([qkv_term, out_term], axis=1).astype(jnp.bfloat16),
        "fsdp",
        scatter_dimension=0,
        tiled=True,
    ).astype(jnp.float32)
    grad_qkv_weight = stacked[:, :qkv_cols]
    grad_out_weight = stacked[:, qkv_cols:]
    partial_back = lax.dot_general(
        grad_qkv, qkv_full, (((1,), (1,)), ((), ())), preferred_element_type=jnp.float32
    )
    summed = lax.psum(partial_back.astype(jnp.bfloat16), "tp").astype(jnp.float32)
    grad_full = norm_back(summed * norm_gain, centred_rows, row_factor)
    grad_share = lax.dynamic_slice_in_dim(grad_full, my_group * share_width, share_width, 1)
    grad_rows = grad_share.astype(jnp.bfloat16)
    return (attended, grad_rows, grad_qkv_weight, grad_out_weight)


def swap_fsdp(value, mask):
    pairs = [(source, source ^ mask) for source in range(lax.axis_size("fsdp"))]
    return lax.ppermute(value, "fsdp", pairs)


def swap_tp(value):
    return lax.ppermute(value, "tp", [(0, 1), (1, 0)])


def send_planes(value, plane_pairs):
    pairs = [
        (source * PLANE + place, target * PLANE + place)
        for source, target in plane_pairs
        for place in range(PLANE)
    ]
    return lax.ppermute(value, "fsdp", pairs)


def after(value, *earlier):
    return lax.optimization_barrier((value,) + earlier)[0]


def spread_places(blocks):
    near = swap_fsdp(jnp.stack([blocks[1], blocks[3]]), 1)
    far = swap_fsdp(jnp.stack([blocks[2], near[1]]), 2)
    return [blocks[0], near[0], far[0], far[1]]


class LineGather:
    def __init__(self, own, my_plane):
        self.own, self.my_plane = (own, my_plane)

    def pair_up(self, *earlier):
        self.partner = swap_fsdp(after(self.own, *earlier), PLANE)

    def cross(self, *earlier):
        even = self.my_plane % 2 == 0
        partner = after(self.partner, *earlier)
        low = jnp.where(even, self.own, partner)
        high = jnp.where(even, partner, self.own)
        self.pair = jnp.concatenate([low, high])
        self.crossed = send_planes(self.pair, [(1, 2), (2, 1)])

    def spread(self, *earlier):
        self.outer = send_planes(after(self.crossed, *earlier), [(1, 0), (2, 3)])

    def whole(self, *earlier):
        inner = (self.my_plane == 1) | (self.my_plane == 2)
        crossed, outer = lax.optimization_barrier((self.crossed, self.outer) + earlier)[:2]
        other = jnp.where(inner, crossed, outer)
        low = self.my_plane < 2
        return jnp.concatenate([jnp.where(low, self.pair, other), jnp.where(low, other, self.pair)])


def pair_up_both(first, second, *earlier):
    both = after(jnp.stack([first.own, second.own]), *earlier)
    both = swap_fsdp(both, PLANE)
    first.partner, second.partner = (both[0], both[1])


def add_rounded(left, right):
    return (left.astype(jnp.float32) + right.astype(jnp.float32)).astype(jnp.bfloat16)


class LineReduce:
    def __init__(self, terms, my_plane):
        self.terms, self.my_plane = (terms, my_plane)
        self.rows = terms[0].shape[1] // 4
        self.far = 2 - 2 * (my_plane // 2)

    def columns(self, start, count):
        return jnp.concatenate(
            [
                lax.dynamic_slice_in_dim(term, start * self.rows, count * self.rows, 1)
                for term in self.terms
            ]
        )

    def inward(self):
        self.sent = self.columns(self.far, 2)
        self.arrived = send_planes(self.sent, [(0, 1), (3, 2)])

    def add_far(self, *earlier):
        far = add_rounded(self.columns(self.far, 2), after(self.arrived, *earlier))
        self.cross_sent = far

    def cross(self, *earlier):
        self.crossed = send_planes(after(self.cross_sent, *earlier), [(1, 2), (2, 1)])

    def of_pair(self, plane, *earlier):
        crossed = after(self.crossed, *earlier)
        crossed = lax.dynamic_slice_in_dim(crossed, plane % 2 * self.rows, self.rows, 1)
        return self.columns(plane, 1).astype(jnp.float32) + crossed.astype(jnp.float32)


class PairReduce:
    def __init__(self, reduces, my_plane, *earlier):
        self.reduces, self.my_plane = (reduces, my_plane)
        sent = jnp.concatenate([reduce.of_pair(my_plane ^ 1, *earlier) for reduce in reduces])
        self.sent = sent.astype(jnp.bfloat16)

    def send(self, *earlier):
        self.got = swap_fsdp(after(self.sent, *earlier), PLANE)

    def total(self, *later):
        kept = [reduce.of_pair(self.my_plane, *later) for reduce in self.reduces]
        got = after(self.got, *later).astype(jnp.float32)
        return (jnp.concatenate(kept) + got).astype(jnp.bfloat16)


def rows_kernel(parts, pick_ref, count_ref, *refs):
    sources, (gain_ref, normed_ref, stats_ref) = (refs[:-3], refs[-3:])
    at = pl.program_id(0)
    rows, half = sources[0].shape[3:]
    width = 2 * half
    live = lax.broadcasted_iota(jnp.int32, (rows, 1), 0) < count_ref[at]
    near = (pick_ref[at] & 1) == 1
    part = at // (pl.num_programs(0) // parts)

    def read(high):
        value = None
        for index in range(parts):
            here, there = sources[4 * index + high], sources[4 * index + 2 + high]
            chosen = jnp.where(near, there[0, 0, 0], here[0, 0, 0])
            value = chosen if value is None else jnp.where(part == index, chosen, value)
        return jnp.where(live, value.astype(jnp.float32), 0.0)

    low = read(0)
    high = read(1)
    mean = (
        jnp.sum(low, axis=-1, keepdims=True) + jnp.sum(high, axis=-1, keepdims=True)
    ) / width
    low = low - mean
    high = high - mean
    variance = (
        jnp.sum(low * low, axis=-1, keepdims=True) + jnp.sum(high * high, axis=-1, keepdims=True)
    ) / width
    factor = lax.rsqrt(variance + epsilon)
    normed_ref[:, :half] = (low * factor * gain_ref[:, :half]).astype(normed_ref.dtype)
    normed_ref[:, half:] = (high * factor * gain_ref[:, half:]).astype(normed_ref.dtype)
    lane = lax.broadcasted_iota(jnp.int32, (rows, stats_ref.shape[1]), 1)
    stats_ref[...] = jnp.where(lane == 0, mean, factor)


def norm_block(here, there, picks, live_counts, norm_gain, my_group):
    parts = len(here)
    _, _, slots, rows, half = here[0].shape
    width = 2 * half
    steps = PLANE * slots
    total = parts * steps
    picks = jnp.concatenate([picks, my_group[None]])

    def source(part, group_xor, near):
        def index(at, pick, count):
            at = jnp.clip(at, part * steps, part * steps + steps - 1)
            first = at // PLANE * PLANE
            stand_in = jnp.where(at - first < 2, first + 2, first + 1)
            chosen = pick[jnp.where((pick[at] & 1) == near, at, stand_in)]
            return (chosen >> 1, pick[total] ^ group_xor, at // PLANE % slots, 0, 0)

        return pl.BlockSpec((1, 1, 1, rows, half), index)

    def target(at, pick, count):
        slot, place = (at // PLANE, at % PLANE)
        return (place * parts * slots + slot, 0)

    arrays, specs = ([], [])
    for part in range(parts):
        arrays += [here[part], here[part], there[part], there[part]]
        specs += [source(part, 0, 0), source(part, 1, 0), source(part, 0, 1), source(part, 1, 1)]
    return pl.pallas_call(
        functools.partial(rows_kernel, parts),
        grid_spec=pltpu.PrefetchScalarGridSpec(
            num_scalar_prefetch=2,
            grid=(total,),
            in_specs=specs + [pl.BlockSpec((1, width), lambda at, pick, count: (0, 0))],
            out_specs=[pl.BlockSpec((rows, width), target), pl.BlockSpec((rows, 128), target)],
        ),
        out_shape=[
            jax.ShapeDtypeStruct((total * rows, width), jnp.bfloat16),
            jax.ShapeDtypeStruct((total * rows, 128), jnp.float32),
        ],
        compiler_params=pltpu.CompilerParams(vmem_limit_bytes=28 * 1024 * 1024),
        cost_estimate=pl.CostEstimate(
            flops=10 * total * rows * width,
            bytes_accessed=6 * total * rows * width,
            transcendentals=0,
        ),
        name="norm_rows",
    )(picks, live_counts, *arrays, norm_gain[None, :])


def mm(left, right, left_dim, right_dim):
    return lax.dot_general(
        left,
        right,
        (((left_dim,), (right_dim,)), ((), ())),
        preferred_element_type=jnp.float32,
    )


def attend_image(projected, grad_mixed, scales, live, rows, head_dim):
    query_hat, query_factor = norm_rows(projected[:, :head_dim])
    key_hat, key_factor = norm_rows(projected[:, head_dim : 2 * head_dim])
    query_scale = scales[0:1, :]
    key_scale = scales[1:2, :]
    query = (query_hat * query_scale).astype(jnp.bfloat16)
    key_rows = (key_hat * key_scale).astype(jnp.bfloat16)
    values = projected[:, 2 * head_dim :].astype(jnp.bfloat16)
    row_id = lax.broadcasted_iota(jnp.int32, (rows, rows), 0)
    col_id = lax.broadcasted_iota(jnp.int32, (rows, rows), 1)
    allowed = ((row_id < live) & (col_id < live)) | (row_id == col_id)
    raised = jnp.where(allowed, jnp.exp(mm(query, key_rows, 1, 1)), 0.0)
    attention = raised / jnp.sum(raised, axis=-1, keepdims=True)
    rounded = attention.astype(jnp.bfloat16)
    mixed = mm(rounded, values, 1, 0).astype(jnp.bfloat16)
    grad_value = mm(rounded, grad_mixed, 0, 0)
    grad_attention = mm(grad_mixed, values, 1, 1)
    grad_scores = attention * (
        grad_attention - jnp.sum(attention * grad_attention, axis=-1, keepdims=True)
    )
    grad_scores = grad_scores.astype(jnp.bfloat16)
    grad_query = mm(grad_scores, key_rows, 1, 0)
    grad_key = mm(grad_scores, query, 0, 0)
    query_grad = norm_back(grad_query * query_scale, query_hat, query_factor)
    key_grad = norm_back(grad_key * key_scale, key_hat, key_factor)
    return (mixed, query_grad, key_grad, grad_value)


def attention_kernel(per_step, count_ref, proj_ref, grad_ref, scale_ref, mixed_ref, back_ref):
    at = pl.program_id(0)
    rows = proj_ref.shape[0] // per_step
    head_dim = grad_ref.shape[1]
    scales = scale_ref[...]
    for image in range(per_step):
        span = slice(image * rows, (image + 1) * rows)
        mixed, query_grad, key_grad, grad_value = attend_image(
            proj_ref[span, :],
            grad_ref[span, :],
            scales,
            count_ref[at * per_step + image],
            rows,
            head_dim,
        )
        mixed_ref[span, :] = mixed
        back_ref[span, :head_dim] = query_grad.astype(jnp.bfloat16)
        back_ref[span, head_dim : 2 * head_dim] = key_grad.astype(jnp.bfloat16)
        back_ref[span, 2 * head_dim :] = grad_value.astype(jnp.bfloat16)


def attend(projected, grad_mixed, scales, live_counts, rows):
    total, head_dim = grad_mixed.shape
    image_count = total // rows
    per_step = 4
    block = per_step * rows
    return pl.pallas_call(
        functools.partial(attention_kernel, per_step),
        grid_spec=pltpu.PrefetchScalarGridSpec(
            num_scalar_prefetch=1,
            grid=(image_count // per_step,),
            in_specs=[
                pl.BlockSpec((block, 3 * head_dim), lambda at, count: (at, 0)),
                pl.BlockSpec((block, head_dim), lambda at, count: (at, 0)),
                pl.BlockSpec((2, head_dim), lambda at, count: (0, 0)),
            ],
            out_specs=[
                pl.BlockSpec((block, head_dim), lambda at, count: (at, 0)),
                pl.BlockSpec((block, 3 * head_dim), lambda at, count: (at, 0)),
            ],
        ),
        out_shape=[
            jax.ShapeDtypeStruct((total, head_dim), jnp.bfloat16),
            jax.ShapeDtypeStruct((total, 3 * head_dim), jnp.bfloat16),
        ],
        compiler_params=pltpu.CompilerParams(vmem_limit_bytes=32 * 1024 * 1024),
        cost_estimate=pl.CostEstimate(
            flops=12 * total * rows * head_dim,
            bytes_accessed=12 * total * head_dim * 2,
            transcendentals=total * rows,
        ),
        name="attend_images",
    )(live_counts, projected, grad_mixed, scales)


class PlaneScatter:
    def __init__(self, sent, share_width, my_group):
        self.share_width, self.my_group = (share_width, my_group)
        self.got = swap_fsdp(sent, 1)

    def mine(self, value):
        start = self.my_group * self.share_width
        return lax.dynamic_slice_in_dim(value, start, self.share_width, value.ndim - 1)

    def other(self, value):
        start = (1 - self.my_group) * self.share_width
        return lax.dynamic_slice_in_dim(value, start, self.share_width, value.ndim - 1)

    def add_cores(self, kept, *earlier):
        got = after(self.got, *earlier) if earlier else self.got
        half = kept.shape[1] // 2
        first = add_rounded(kept[:, :half], got[:, :half])
        near = add_rounded(kept[0, half:], got[0, half:])
        far = add_rounded(kept[1, half:], got[1, half:])
        self.first, self.near = (first, near)
        sent_x = self.other(first)
        self.over_x = swap_tp(sent_x)
        self.over_y = swap_fsdp(far, 2)
        return (first, far, sent_x)

    def turn(self, *earlier):
        over_x = after(self.over_x, *earlier)
        over_y = after(self.over_y, *earlier)
        first = self.mine(self.first).astype(jnp.float32) + over_x.astype(jnp.float32)
        second = self.near.astype(jnp.float32) + over_y.astype(jnp.float32)
        self.first_sum = first[0]
        self.second_sum = self.mine(second)
        sent_y = first[1].astype(jnp.bfloat16)
        sent_x = self.other(second).astype(jnp.bfloat16)
        self.last_y = swap_fsdp(sent_y, 2)
        self.last_x = swap_tp(sent_x)
        return (sent_y, sent_x)

    def total(self):
        return jnp.concatenate(
            [
                self.first_sum + self.last_y.astype(jnp.float32),
                self.second_sum + self.last_x.astype(jnp.float32),
            ]
        )


def home_kernel(counts, place_ref, *refs):
    qkv_ref, out_ref = refs[-2:]
    at, head = (pl.program_id(0), pl.program_id(1))
    width = qkv_ref.shape[1]
    first = 0
    for group, count in enumerate(counts):
        inside = (head >= first) & (head < first + count)
        for step in range(PLANE):

            @pl.when((at == step) & inside)
            def _():
                value = refs[group * PLANE + step][...].astype(jnp.float32)
                qkv_ref[...] = value[:, :width]
                out_ref[...] = value[:, width:]

        first += count


def place_home(groups, my_place, heads, head_dim):
    rows = groups[0][0].shape[0]
    head_width = 4 * head_dim
    qkv_width = 3 * head_dim
    counts = [blocks[0].shape[1] // head_width for blocks in groups]

    def source(first, count):
        return pl.BlockSpec(
            (rows, head_width), lambda at, head, place: (0, jnp.clip(head - first, 0, count - 1))
        )

    specs = []
    for group, count in enumerate(counts):
        specs += [source(sum(counts[:group]), count)] * PLANE

    def target(at, head, place):
        return (0, (place[0] ^ at) * heads + head)

    total = PLANE * heads
    return pl.pallas_call(
        functools.partial(home_kernel, counts),
        grid_spec=pltpu.PrefetchScalarGridSpec(
            num_scalar_prefetch=1,
            grid=(PLANE, heads),
            in_specs=specs,
            out_specs=[
                pl.BlockSpec((rows, qkv_width), target),
                pl.BlockSpec((rows, head_dim), target),
            ],
        ),
        out_shape=[
            jax.ShapeDtypeStruct((rows, total * qkv_width), jnp.float32),
            jax.ShapeDtypeStruct((rows, total * head_dim), jnp.float32),
        ],
        compiler_params=pltpu.CompilerParams(vmem_limit_bytes=32 * 1024 * 1024),
        cost_estimate=pl.CostEstimate(
            flops=total * rows * head_width,
            bytes_accessed=6 * total * rows * head_width,
            transcendentals=0,
        ),
        name="place_home",
    )(my_place[None], *[block for blocks in groups for block in blocks])


def per_plane(patches, cotangent, counts, masks, norm_gain, qk_gain, qkv_weight, out_weight):
    replicas = lax.axis_size("fsdp")
    groups = lax.axis_size("tp")
    planes = replicas // PLANE
    my_replica = lax.axis_index("fsdp")
    my_group = lax.axis_index("tp")
    my_plane = my_replica // PLANE
    my_place = lax.rem(my_replica, PLANE)
    tok_rows = patches.shape[0]
    images = counts.shape[1]
    slot_rows = tok_rows // images
    model_width = norm_gain.shape[0]
    share_width = model_width // groups
    head_dim = qk_gain.shape[1]
    shard_rows = qkv_weight.shape[0]
    local_heads = out_weight.shape[1] // head_dim
    heads = local_heads // PLANE
    qkv_width = 3 * head_dim
    head_width = 4 * head_dim
    parts = 2
    slots = images // parts
    part_rows = slots * slot_rows

    replica_ids = jnp.arange(replicas, dtype=jnp.int32)
    relative = jnp.array(ORDER, dtype=jnp.int32)
    own_at = ORDER.index(0)
    sources = (my_replica ^ relative)[:, None] ^ masks[None, :]
    live_counts = jnp.sum(
        jnp.where(replica_ids[:, None, None] == sources[None], counts[:, None, :], 0), axis=0
    ).astype(jnp.int32)
    picks = (relative[:, None] ^ (masks & (PLANE - 1))[None, :]).astype(jnp.int32)
    places = jnp.arange(slot_rows, dtype=jnp.int32)
    is_live = (places[None, :] < live_counts[own_at][:, None]).reshape(tok_rows)

    def by_part(table):
        return jnp.transpose(table).reshape(-1)

    flat_counts = live_counts.reshape(-1)

    holding = lax.dynamic_slice_in_dim(patches, my_group * share_width, share_width, 1)
    holding = holding.reshape(parts, slots, slot_rows, share_width)
    moved = [holding[part] for part in range(parts)]
    first_moved = None
    for bit_place in range(2, replicas.bit_length() - 1):
        previous = None
        for part in range(parts):
            piece = moved[part] if previous is None else after(moved[part], previous)
            partner = swap_fsdp(piece, 2**bit_place)
            moving = jnp.right_shift(masks[part * slots : (part + 1) * slots], bit_place) & 1
            moved[part] = jnp.where((moving == 1)[:, None, None], partner, moved[part])
            previous = partner
            if first_moved is None:
                first_moved = moved[0]
            if part == 0:
                first_there = partner
            if part == 1 and bit_place == 2:
                second_moved = moved[1]

    def head_columns(place):
        qkv_part = lax.dynamic_slice_in_dim(
            qkv_weight, place * heads * qkv_width, heads * qkv_width, 1
        )
        out_part = lax.dynamic_slice_in_dim(
            out_weight, place * heads * head_dim, heads * head_dim, 1
        )
        return jnp.concatenate([qkv_part, out_part], axis=1)

    upstream_own = jnp.where(is_live[:, None], cotangent, jnp.zeros((), cotangent.dtype))
    up_far = [swap_fsdp(upstream_own[:part_rows], 2)]
    up_near = swap_fsdp(after(upstream_own, first_moved), 1)
    shards = spread_places([head_columns(my_place ^ step) for step in range(PLANE)])
    shards = [after(shard, first_moved, up_near, up_far[0]) for shard in shards]
    plane_shard = jnp.zeros((PLANE, shard_rows, heads * head_width), qkv_weight.dtype)
    for step in range(PLANE):
        plane_shard = lax.dynamic_update_index_in_dim(
            plane_shard, shards[step], my_place ^ step, 0
        )
    plane_shard = plane_shard.reshape(PLANE * shard_rows, heads * head_width)
    shards_of = []
    for head in range(heads):
        qkv_at = head * qkv_width
        out_at = heads * qkv_width + head * head_dim
        shard = jnp.concatenate(
            [
                plane_shard[:, qkv_at : qkv_at + qkv_width],
                plane_shard[:, out_at : out_at + head_dim],
            ],
            axis=1,
        )
        shards_of.append(shard)

    gathers = [LineGather(shard, my_plane) for shard in shards_of]
    gathers[0].pair_up(first_there)
    gathers[0].cross(moved[-1])

    here, there = ([], [])
    for part in range(parts):
        own = moved[part]
        over = swap_tp(own)
        if part == 0:
            far = swap_fsdp(after(own, second_moved, *shards), 2)
            far_over = swap_tp(far)
        else:
            far = swap_fsdp(after(own, gathers[0].partner), 2)
            far_over = swap_tp(after(far, over, here[0]))
            pair_up_both(gathers[1], gathers[2], gathers[0].partner)
            up_far.append(swap_fsdp(after(upstream_own[part_rows:], far), 2))
            own = after(own, gathers[0].crossed, gathers[1].partner)
        here.append(
            jnp.stack([own, over, far, far_over]).reshape(
                2, 2, slots, slot_rows, share_width
            )
        )
        there.append(swap_fsdp(here[part], 1))
    gathers[0].spread()
    gathers[1].cross()

    normed, stats = norm_block(
        here,
        there,
        by_part(picks),
        by_part(live_counts),
        norm_gain,
        my_group,
    )
    gathers[1].spread(normed)
    gathers[2].cross(normed)
    up_far[1] = after(up_far[1], normed)
    up_both = [swap_fsdp(after(up_far[0], normed), 1), swap_fsdp(up_far[1], 1)]
    upstream = jnp.concatenate([up_near, *up_both, upstream_own, *up_far])

    scales = jnp.concatenate([qk_gain[0:1] * head_dim ** (-0.5), qk_gain[1:2]])
    weights, mixed_parts, back_parts, reduces = ([], [], [], [])
    for head in range(heads):
        if head == 0:
            weight = gathers[0].whole(normed, gathers[1].crossed, gathers[2].partner)
        elif head == 1:
            weight = gathers[1].whole(qkv_term, out_term, gathers[2].crossed)
            gathers[2].spread(qkv_term)
        else:
            weight = gathers[2].whole(qkv_term, out_term, reduces[0].cross_sent)
        weights.append(weight)
        grad_mixed = mm(upstream, weight[:, qkv_width:], 1, 0).astype(jnp.bfloat16)
        projected = mm(normed, weight[:, :qkv_width], 1, 0)
        mixed, back = attend(projected, grad_mixed, scales, flat_counts, slot_rows)
        mixed_parts.append(mixed)
        back_parts.append(back)
        held_back, held_mixed = (back, mixed)
        if head == 2:
            mixed_all = after(
                jnp.concatenate(mixed_parts, axis=1), reduces[1].arrived, reduces[0].crossed
            )
            out_all = jnp.concatenate([weight[:, qkv_width:] for weight in weights], axis=1)
            out_sent = mm(mixed_all[: 2 * tok_rows], out_all, 1, 1).astype(jnp.bfloat16)
            out_scatter = PlaneScatter(
                out_sent.reshape(2, tok_rows, model_width), share_width, my_group
            )
            reduces[1].add_far(out_sent)
            reduces[1].cross()
            held = after(mixed_all[2 * tok_rows :], out_sent, reduces[1].cross_sent)
            out_kept = mm(held, out_all, 1, 1).astype(jnp.bfloat16)
            held_back = after(held_back, out_kept)
            held_mixed = after(held_mixed, out_kept)
        qkv_term = mm(held_back, normed, 0, 0).astype(jnp.bfloat16)
        out_term = mm(held_mixed, upstream, 0, 0).astype(jnp.bfloat16)
        if head == 1:
            reduces[0].add_far(qkv_term, out_term)
            reduces[0].cross()
        reduces.append(LineReduce([qkv_term, out_term], my_plane))
        reduces[head].inward()

    def send_home(total):
        count = total.shape[0] // head_width
        summed = total.T.reshape(PLANE, shard_rows, count * head_width)
        return spread_places(
            [
                lax.dynamic_index_in_dim(summed, my_place ^ step, 0, keepdims=False)
                for step in range(PLANE)
            ]
        )

    back_all = jnp.concatenate(back_parts, axis=1)
    qkv_all = jnp.concatenate([weight[:, :qkv_width] for weight in weights], axis=1)
    out_added = out_scatter.add_cores(
        after(out_kept.reshape(2, tok_rows, model_width), qkv_term, out_term)
    )
    held = after(back_all[: 2 * tok_rows], *out_added, reduces[2].sent)
    back_sent = mm(held, qkv_all, 1, 1).astype(jnp.bfloat16)
    reduces[2].add_far(back_sent)
    early = PairReduce(reduces[:2], my_plane, back_sent)
    between = (reduces[2].cross_sent, early.sent)
    back_scatter = PlaneScatter(
        after(
            back_sent.reshape(2, tok_rows, model_width),
            out_scatter.over_x,
            out_scatter.over_y,
            *between,
        ),
        share_width,
        my_group,
    )
    turned = out_scatter.turn(*between)
    reduces[2].cross(*turned)
    early.send(*turned)
    held = after(back_all[2 * tok_rows :], *turned)
    back_kept = mm(held, qkv_all, 1, 1).astype(jnp.bfloat16)
    back_added = back_scatter.add_cores(
        after(
            back_kept.reshape(2, tok_rows, model_width),
            out_scatter.last_x,
            out_scatter.last_y,
            reduces[2].crossed,
        )
    )
    late = PairReduce(reduces[2:], my_plane, *back_added)
    late.send()
    turned = back_scatter.turn(late.sent)
    total = jnp.concatenate([early.total(*back_added), late.total(*turned)])
    home = send_home(after(total, *turned))
    attended = out_scatter.total()
    attended = jnp.where(is_live[:, None], attended, 0.0).astype(jnp.bfloat16)
    grad_normed = back_scatter.total()

    def own_slot(part, slot):
        pick = picks[own_at, part * slots + slot]
        mine = lax.dynamic_index_in_dim(here[part][:, 0, slot], pick >> 1, 0, keepdims=False)
        other = lax.dynamic_index_in_dim(there[part][:, 0, slot], pick >> 1, 0, keepdims=False)
        return jnp.where((pick & 1) == 1, other, mine)

    own_rows = jnp.concatenate(
        [own_slot(part, slot) for part in range(parts) for slot in range(slots)]
    ).astype(jnp.float32)
    own_rows = jnp.where(is_live[:, None], own_rows, 0.0)
    own_stats = stats[own_at * tok_rows : (own_at + 1) * tok_rows, 0:2]
    mean = own_stats[:, 0:1]
    factor = own_stats[:, 1:2]
    centred = (own_rows - mean) * factor
    gain_share = lax.dynamic_slice_in_dim(norm_gain, my_group * share_width, share_width, 0)
    weighted = grad_normed * gain_share
    sums = jnp.stack([jnp.sum(weighted, axis=-1), jnp.sum(weighted * centred, axis=-1)])
    sums = (sums + swap_tp(sums)) / model_width
    grad_rows = factor * (weighted - sums[0][:, None] - centred * sums[1][:, None])
    grad_rows = grad_rows.astype(jnp.bfloat16)

    grad_qkv_weight, grad_out_weight = place_home([home], my_place, heads, head_dim)
    return (attended, grad_rows, grad_qkv_weight, grad_out_weight)


def solution(mesh):
    def body(patches, cotangent, counts, masks, norm_gain, qk_gain, qkv_weight, out_weight):
        replicas = mesh.shape["fsdp"]
        local_heads = out_weight.shape[1] // qk_gain.shape[1]
        planar = (
            mesh.shape["tp"] == 2
            and replicas == 4 * PLANE
            and replicas & (replicas - 1) == 0
            and local_heads == 3 * PLANE
            and qk_gain.shape[1] == 128
            and counts.shape[1] == 4
        )
        plan = per_plane if planar else per_device
        return plan(
            patches, cotangent, counts, masks, norm_gain, qk_gain, qkv_weight, out_weight
        )

    in_specs = (
        P("fsdp", None),
        P("fsdp", None),
        P(),
        P(),
        P(),
        P(),
        P("fsdp", "tp"),
        P("fsdp", "tp"),
    )
    out_specs = (P("fsdp", "tp"), P("fsdp", "tp"), P("fsdp", "tp"), P("fsdp", "tp"))
    return jax.shard_map(
        body, mesh=mesh, in_specs=in_specs, out_specs=out_specs, check_vma=False
    )
```

```python
import functools
import jax
import jax.numpy as jnp
from jax import lax
from jax.experimental import pallas as pl
from jax.experimental.pallas import tpu as pltpu
from jax.sharding import PartitionSpec as P

epsilon = 1e-06
PLANE = 4
ORDER = (1, 3, 0, 2)


def partner_2(value, axis, stride):
    mask = 2**stride
    pairs = [(source, source ^ mask) for source in range(lax.axis_size(axis))]
    return lax.ppermute(value, axis, pairs)


def norm_rows(values):
    row_mean = jnp.mean(values, axis=-1, keepdims=True)
    centred = values - row_mean
    factor = lax.rsqrt(jnp.mean(centred * centred, axis=-1, keepdims=True) + epsilon)
    return (centred * factor, factor)


def norm_back(upstream, normed, factor):
    return factor * (
        upstream
        - jnp.mean(upstream, axis=-1, keepdims=True)
        - normed * jnp.mean(upstream * normed, axis=-1, keepdims=True)
    )


def per_device(patches, cotangent, counts, masks, norm_gain, qk_gain, qkv_weight, out_weight):
    replicas = lax.axis_size("fsdp")
    groups = lax.axis_size("tp")
    my_replica = lax.axis_index("fsdp")
    my_group = lax.axis_index("tp")
    tok_rows = patches.shape[0]
    images = counts.shape[1]
    slot_rows = tok_rows // images
    model_width = norm_gain.shape[0]
    share_width = model_width // groups
    head_dim = qk_gain.shape[1]
    qkv_cols = qkv_weight.shape[1]
    out_cols = out_weight.shape[1]
    local_heads = out_cols // head_dim
    row_slot = jnp.arange(tok_rows, dtype=jnp.int32) // slot_rows
    holding = lax.dynamic_slice_in_dim(patches, my_group * share_width, share_width, 1)
    digit_count = replicas.bit_length() - 1
    digit_order = list(range(digit_count))
    for bit_place in digit_order:
        partner = partner_2(holding, "fsdp", bit_place)
        moving = jnp.bitwise_and(jnp.right_shift(masks, bit_place), 1) == 1
        take_rows = jnp.take(moving, row_slot)
        holding = jnp.where(take_rows[:, None], partner, holding)
    replica_ids = jnp.arange(replicas, dtype=jnp.int32)
    sources = jnp.bitwise_xor(my_replica, masks)
    run_counts = jnp.sum(jnp.where(replica_ids[:, None] == sources[None, :], counts, 0), axis=0)
    places = jnp.arange(slot_rows, dtype=jnp.int32)
    live_slots = places[None, :] < run_counts[:, None]
    is_live = live_slots.reshape(tok_rows)
    allowed = live_slots[:, :, None] & live_slots[:, None, :] | jnp.eye(slot_rows, dtype=bool)[None]
    packed = jnp.where(is_live[:, None], holding, jnp.zeros((), holding.dtype))
    block_rows = lax.all_gather(packed, "tp", axis=1, tiled=True)
    qkv_full, out_full = (
        lax.all_gather(qkv_weight, "fsdp", axis=0, tiled=True),
        lax.all_gather(out_weight, "fsdp", axis=0, tiled=True),
    )
    centred_rows, row_factor = norm_rows(block_rows.astype(jnp.float32))
    normed = (centred_rows * norm_gain).astype(jnp.bfloat16)
    projected = jnp.dot(normed, qkv_full, preferred_element_type=jnp.float32).reshape(
        images, slot_rows, local_heads, 3, head_dim
    )
    query_hat, query_factor = norm_rows(projected[:, :, :, 0])
    key_hat, key_factor = norm_rows(projected[:, :, :, 1])
    query_scale = qk_gain[0] * head_dim ** (-0.5)
    key_scale = qk_gain[1]
    query = (query_hat * query_scale).astype(jnp.bfloat16)
    key_rows = (key_hat * key_scale).astype(jnp.bfloat16)
    values = projected[:, :, :, 2].astype(jnp.bfloat16)
    scores = jnp.einsum("sqhe,skhe->shqk", query, key_rows, preferred_element_type=jnp.float32)
    raised = jnp.where(allowed[:, None], jnp.exp(scores), 0.0)
    attention = raised / jnp.sum(raised, axis=-1, keepdims=True)
    rounded_attention = attention.astype(jnp.bfloat16)
    mixed = jnp.einsum(
        "shqk,skhe->sqhe", rounded_attention, values, preferred_element_type=jnp.float32
    )
    mixed = mixed.astype(jnp.bfloat16).reshape(tok_rows, out_cols)
    partial_value = lax.dot_general(
        mixed, out_full, (((1,), (1,)), ((), ())), preferred_element_type=jnp.float32
    )
    attended = lax.psum_scatter(
        partial_value.astype(jnp.bfloat16), "tp", scatter_dimension=1, tiled=True
    ).astype(jnp.float32)
    attended = jnp.where(is_live[:, None], attended, 0.0).astype(jnp.bfloat16)
    upstream_rows = jnp.where(is_live[:, None], cotangent, jnp.zeros((), cotangent.dtype))
    grad_mixed = jnp.dot(upstream_rows, out_full, preferred_element_type=jnp.float32).astype(
        jnp.bfloat16
    )
    grad_heads = grad_mixed.reshape(images, slot_rows, local_heads, head_dim)
    grad_value = jnp.einsum(
        "shqk,sqhe->skhe", rounded_attention, grad_heads, preferred_element_type=jnp.float32
    )
    grad_attention = jnp.einsum(
        "sqhe,skhe->shqk", grad_heads, values, preferred_element_type=jnp.float32
    )
    grad_scores = attention * (
        grad_attention - jnp.sum(attention * grad_attention, axis=-1, keepdims=True)
    )
    grad_scores = grad_scores.astype(jnp.bfloat16)
    grad_query = jnp.einsum(
        "shqk,skhe->sqhe", grad_scores, key_rows, preferred_element_type=jnp.float32
    )
    grad_key = jnp.einsum("shqk,sqhe->skhe", grad_scores, query, preferred_element_type=jnp.float32)
    query_grad = norm_back(grad_query * query_scale, query_hat, query_factor)
    key_grad = norm_back(grad_key * key_scale, key_hat, key_factor)
    grad_qkv = (
        jnp.stack([query_grad, key_grad, grad_value], axis=3)
        .astype(jnp.bfloat16)
        .reshape(tok_rows, qkv_cols)
    )
    qkv_term = lax.dot_general(
        normed, grad_qkv, (((0,), (0,)), ((), ())), preferred_element_type=jnp.float32
    )
    out_term = lax.dot_general(
        upstream_rows, mixed, (((0,), (0,)), ((), ())), preferred_element_type=jnp.float32
    )
    stacked = lax.psum_scatter(
        jnp.concatenate([qkv_term, out_term], axis=1).astype(jnp.bfloat16),
        "fsdp",
        scatter_dimension=0,
        tiled=True,
    ).astype(jnp.float32)
    grad_qkv_weight = stacked[:, :qkv_cols]
    grad_out_weight = stacked[:, qkv_cols:]
    partial_back = lax.dot_general(
        grad_qkv, qkv_full, (((1,), (1,)), ((), ())), preferred_element_type=jnp.float32
    )
    summed = lax.psum(partial_back.astype(jnp.bfloat16), "tp").astype(jnp.float32)
    grad_full = norm_back(summed * norm_gain, centred_rows, row_factor)
    grad_share = lax.dynamic_slice_in_dim(grad_full, my_group * share_width, share_width, 1)
    grad_rows = grad_share.astype(jnp.bfloat16)
    return (attended, grad_rows, grad_qkv_weight, grad_out_weight)


def swap_fsdp(value, mask):
    pairs = [(source, source ^ mask) for source in range(lax.axis_size("fsdp"))]
    return lax.ppermute(value, "fsdp", pairs)


def swap_tp(value):
    return lax.ppermute(value, "tp", [(0, 1), (1, 0)])


def send_planes(value, plane_pairs):
    pairs = [
        (source * PLANE + place, target * PLANE + place)
        for source, target in plane_pairs
        for place in range(PLANE)
    ]
    return lax.ppermute(value, "fsdp", pairs)


def after(value, *earlier):
    return lax.optimization_barrier((value,) + earlier)[0]


def spread_places(blocks):
    near = swap_fsdp(jnp.stack([blocks[1], blocks[3]]), 1)
    far = swap_fsdp(jnp.stack([blocks[2], near[1]]), 2)
    return [blocks[0], near[0], far[0], far[1]]


class LineGather:
    def __init__(self, own, my_plane):
        self.own, self.my_plane = (own, my_plane)

    def pair_up(self, *earlier):
        self.partner = swap_fsdp(after(self.own, *earlier), PLANE)

    def cross(self, *earlier):
        even = self.my_plane % 2 == 0
        partner = after(self.partner, *earlier)
        low = jnp.where(even, self.own, partner)
        high = jnp.where(even, partner, self.own)
        self.pair = jnp.concatenate([low, high])
        self.crossed = send_planes(self.pair, [(1, 2), (2, 1)])

    def spread(self, *earlier):
        self.outer = send_planes(after(self.crossed, *earlier), [(1, 0), (2, 3)])

    def whole(self, *earlier):
        inner = (self.my_plane == 1) | (self.my_plane == 2)
        crossed, outer = lax.optimization_barrier((self.crossed, self.outer) + earlier)[:2]
        other = jnp.where(inner, crossed, outer)
        low = self.my_plane < 2
        return jnp.concatenate([jnp.where(low, self.pair, other), jnp.where(low, other, self.pair)])


def pair_up_both(first, second, *earlier):
    both = after(jnp.stack([first.own, second.own]), *earlier)
    both = swap_fsdp(both, PLANE)
    first.partner, second.partner = (both[0], both[1])


def add_rounded(left, right):
    return (left.astype(jnp.float32) + right.astype(jnp.float32)).astype(jnp.bfloat16)


class LineReduce:
    def __init__(self, terms, my_plane):
        self.terms, self.my_plane = (terms, my_plane)
        self.rows = terms[0].shape[1] // 4
        self.far = 2 - 2 * (my_plane // 2)

    def columns(self, start, count):
        return jnp.concatenate(
            [
                lax.dynamic_slice_in_dim(term, start * self.rows, count * self.rows, 1)
                for term in self.terms
            ]
        )

    def inward(self):
        self.sent = self.columns(self.far, 2)
        self.arrived = send_planes(self.sent, [(0, 1), (3, 2)])

    def add_far(self, *earlier):
        far = add_rounded(self.columns(self.far, 2), after(self.arrived, *earlier))
        self.cross_sent = far

    def cross(self, *earlier):
        self.crossed = send_planes(after(self.cross_sent, *earlier), [(1, 2), (2, 1)])

    def of_pair(self, plane, *earlier):
        crossed = after(self.crossed, *earlier)
        crossed = lax.dynamic_slice_in_dim(crossed, plane % 2 * self.rows, self.rows, 1)
        return self.columns(plane, 1).astype(jnp.float32) + crossed.astype(jnp.float32)


class PairReduce:
    def __init__(self, reduces, my_plane, *earlier):
        self.reduces, self.my_plane = (reduces, my_plane)
        sent = jnp.concatenate([reduce.of_pair(my_plane ^ 1, *earlier) for reduce in reduces])
        self.sent = sent.astype(jnp.bfloat16)

    def send(self, *earlier):
        self.got = swap_fsdp(after(self.sent, *earlier), PLANE)

    def total(self, *later):
        kept = [reduce.of_pair(self.my_plane, *later) for reduce in self.reduces]
        got = after(self.got, *later).astype(jnp.float32)
        return (jnp.concatenate(kept) + got).astype(jnp.bfloat16)


def rows_kernel(parts, pick_ref, count_ref, *refs):
    sources, (gain_ref, normed_ref, stats_ref) = (refs[:-3], refs[-3:])
    at = pl.program_id(0)
    rows, half = sources[0].shape[3:]
    width = 2 * half
    live = lax.broadcasted_iota(jnp.int32, (rows, 1), 0) < count_ref[at]
    near = (pick_ref[at] & 1) == 1
    part = at // (pl.num_programs(0) // parts)

    def read(high):
        value = None
        for index in range(parts):
            here, there = sources[4 * index + high], sources[4 * index + 2 + high]
            chosen = jnp.where(near, there[0, 0, 0], here[0, 0, 0])
            value = chosen if value is None else jnp.where(part == index, chosen, value)
        return jnp.where(live, value.astype(jnp.float32), 0.0)

    low = read(0)
    high = read(1)
    mean = (
        jnp.sum(low, axis=-1, keepdims=True) + jnp.sum(high, axis=-1, keepdims=True)
    ) / width
    low = low - mean
    high = high - mean
    variance = (
        jnp.sum(low * low, axis=-1, keepdims=True) + jnp.sum(high * high, axis=-1, keepdims=True)
    ) / width
    factor = lax.rsqrt(variance + epsilon)
    normed_ref[:, :half] = (low * factor * gain_ref[:, :half]).astype(normed_ref.dtype)
    normed_ref[:, half:] = (high * factor * gain_ref[:, half:]).astype(normed_ref.dtype)
    lane = lax.broadcasted_iota(jnp.int32, (rows, stats_ref.shape[1]), 1)
    stats_ref[...] = jnp.where(lane == 0, mean, factor)


def norm_block(here, there, picks, live_counts, norm_gain, my_group):
    parts = len(here)
    _, _, slots, rows, half = here[0].shape
    width = 2 * half
    steps = PLANE * slots
    total = parts * steps
    picks = jnp.concatenate([picks, my_group[None]])

    def source(part, group_xor, near):
        def index(at, pick, count):
            at = jnp.clip(at, part * steps, part * steps + steps - 1)
            first = at // PLANE * PLANE
            stand_in = jnp.where(at - first < 2, first + 2, first + 1)
            chosen = pick[jnp.where((pick[at] & 1) == near, at, stand_in)]
            return (chosen >> 1, pick[total] ^ group_xor, at // PLANE % slots, 0, 0)

        return pl.BlockSpec((1, 1, 1, rows, half), index)

    def target(at, pick, count):
        slot, place = (at // PLANE, at % PLANE)
        return (place * parts * slots + slot, 0)

    arrays, specs = ([], [])
    for part in range(parts):
        arrays += [here[part], here[part], there[part], there[part]]
        specs += [source(part, 0, 0), source(part, 1, 0), source(part, 0, 1), source(part, 1, 1)]
    return pl.pallas_call(
        functools.partial(rows_kernel, parts),
        grid_spec=pltpu.PrefetchScalarGridSpec(
            num_scalar_prefetch=2,
            grid=(total,),
            in_specs=specs + [pl.BlockSpec((1, width), lambda at, pick, count: (0, 0))],
            out_specs=[pl.BlockSpec((rows, width), target), pl.BlockSpec((rows, 128), target)],
        ),
        out_shape=[
            jax.ShapeDtypeStruct((total * rows, width), jnp.bfloat16),
            jax.ShapeDtypeStruct((total * rows, 128), jnp.float32),
        ],
        compiler_params=pltpu.CompilerParams(vmem_limit_bytes=28 * 1024 * 1024),
        cost_estimate=pl.CostEstimate(
            flops=10 * total * rows * width,
            bytes_accessed=6 * total * rows * width,
            transcendentals=0,
        ),
        name="norm_rows",
    )(picks, live_counts, *arrays, norm_gain[None, :])


def mm(left, right, left_dim, right_dim):
    return lax.dot_general(
        left,
        right,
        (((left_dim,), (right_dim,)), ((), ())),
        preferred_element_type=jnp.float32,
    )


def attend_image(projected, grad_mixed, scales, live, rows, head_dim):
    query_hat, query_factor = norm_rows(projected[:, :head_dim])
    key_hat, key_factor = norm_rows(projected[:, head_dim : 2 * head_dim])
    query_scale = scales[0:1, :]
    key_scale = scales[1:2, :]
    query = (query_hat * query_scale).astype(jnp.bfloat16)
    key_rows = (key_hat * key_scale).astype(jnp.bfloat16)
    values = projected[:, 2 * head_dim :].astype(jnp.bfloat16)
    row_id = lax.broadcasted_iota(jnp.int32, (rows, rows), 0)
    col_id = lax.broadcasted_iota(jnp.int32, (rows, rows), 1)
    allowed = ((row_id < live) & (col_id < live)) | (row_id == col_id)
    raised = jnp.where(allowed, jnp.exp(mm(query, key_rows, 1, 1)), 0.0)
    attention = raised / jnp.sum(raised, axis=-1, keepdims=True)
    rounded = attention.astype(jnp.bfloat16)
    mixed = mm(rounded, values, 1, 0).astype(jnp.bfloat16)
    grad_value = mm(rounded, grad_mixed, 0, 0)
    grad_attention = mm(grad_mixed, values, 1, 1)
    grad_scores = attention * (
        grad_attention - jnp.sum(attention * grad_attention, axis=-1, keepdims=True)
    )
    grad_scores = grad_scores.astype(jnp.bfloat16)
    grad_query = mm(grad_scores, key_rows, 1, 0)
    grad_key = mm(grad_scores, query, 0, 0)
    query_grad = norm_back(grad_query * query_scale, query_hat, query_factor)
    key_grad = norm_back(grad_key * key_scale, key_hat, key_factor)
    return (mixed, query_grad, key_grad, grad_value)


def attention_kernel(per_step, count_ref, proj_ref, grad_ref, scale_ref, mixed_ref, back_ref):
    at = pl.program_id(0)
    rows = proj_ref.shape[0] // per_step
    head_dim = grad_ref.shape[1]
    scales = scale_ref[...]
    for image in range(per_step):
        span = slice(image * rows, (image + 1) * rows)
        mixed, query_grad, key_grad, grad_value = attend_image(
            proj_ref[span, :],
            grad_ref[span, :],
            scales,
            count_ref[at * per_step + image],
            rows,
            head_dim,
        )
        mixed_ref[span, :] = mixed
        back_ref[span, :head_dim] = query_grad.astype(jnp.bfloat16)
        back_ref[span, head_dim : 2 * head_dim] = key_grad.astype(jnp.bfloat16)
        back_ref[span, 2 * head_dim :] = grad_value.astype(jnp.bfloat16)


def attend(projected, grad_mixed, scales, live_counts, rows):
    total, head_dim = grad_mixed.shape
    image_count = total // rows
    per_step = 4
    block = per_step * rows
    return pl.pallas_call(
        functools.partial(attention_kernel, per_step),
        grid_spec=pltpu.PrefetchScalarGridSpec(
            num_scalar_prefetch=1,
            grid=(image_count // per_step,),
            in_specs=[
                pl.BlockSpec((block, 3 * head_dim), lambda at, count: (at, 0)),
                pl.BlockSpec((block, head_dim), lambda at, count: (at, 0)),
                pl.BlockSpec((2, head_dim), lambda at, count: (0, 0)),
            ],
            out_specs=[
                pl.BlockSpec((block, head_dim), lambda at, count: (at, 0)),
                pl.BlockSpec((block, 3 * head_dim), lambda at, count: (at, 0)),
            ],
        ),
        out_shape=[
            jax.ShapeDtypeStruct((total, head_dim), jnp.bfloat16),
            jax.ShapeDtypeStruct((total, 3 * head_dim), jnp.bfloat16),
        ],
        compiler_params=pltpu.CompilerParams(vmem_limit_bytes=32 * 1024 * 1024),
        cost_estimate=pl.CostEstimate(
            flops=12 * total * rows * head_dim,
            bytes_accessed=12 * total * head_dim * 2,
            transcendentals=total * rows,
        ),
        name="attend_images",
    )(live_counts, projected, grad_mixed, scales)


class PlaneScatter:
    def __init__(self, sent, share_width, my_group):
        self.share_width, self.my_group = (share_width, my_group)
        self.got = swap_fsdp(sent, 1)

    def mine(self, value):
        start = self.my_group * self.share_width
        return lax.dynamic_slice_in_dim(value, start, self.share_width, value.ndim - 1)

    def other(self, value):
        start = (1 - self.my_group) * self.share_width
        return lax.dynamic_slice_in_dim(value, start, self.share_width, value.ndim - 1)

    def add_cores(self, kept, *earlier):
        got = after(self.got, *earlier) if earlier else self.got
        half = kept.shape[1] // 2
        first = add_rounded(kept[:, :half], got[:, :half])
        near = add_rounded(kept[0, half:], got[0, half:])
        far = add_rounded(kept[1, half:], got[1, half:])
        self.first, self.near = (first, near)
        sent_x = self.other(first)
        self.over_x = swap_tp(sent_x)
        self.over_y = swap_fsdp(far, 2)
        return (first, far, sent_x)

    def turn(self, *earlier):
        over_x = after(self.over_x, *earlier)
        over_y = after(self.over_y, *earlier)
        first = self.mine(self.first).astype(jnp.float32) + over_x.astype(jnp.float32)
        second = self.near.astype(jnp.float32) + over_y.astype(jnp.float32)
        self.first_sum = first[0]
        self.second_sum = self.mine(second)
        sent_y = first[1].astype(jnp.bfloat16)
        sent_x = self.other(second).astype(jnp.bfloat16)
        self.last_y = swap_fsdp(sent_y, 2)
        self.last_x = swap_tp(sent_x)
        return (sent_y, sent_x)

    def total(self):
        return jnp.concatenate(
            [
                self.first_sum + self.last_y.astype(jnp.float32),
                self.second_sum + self.last_x.astype(jnp.float32),
            ]
        )


def home_kernel(heads, place_ref, *refs):
    block_refs, (qkv_ref, out_ref) = (refs[:PLANE], refs[-2:])
    at = pl.program_id(0)
    qkv_width = qkv_ref.shape[1] // heads
    head_dim = out_ref.shape[1] // heads
    head_width = qkv_width + head_dim
    for step in range(PLANE):

        @pl.when(at == step)
        def _():
            for head in range(heads):
                low = head * head_width
                value = block_refs[step][:, low : low + head_width].astype(jnp.float32)
                qkv_ref[:, head * qkv_width : (head + 1) * qkv_width] = value[:, :qkv_width]
                out_ref[:, head * head_dim : (head + 1) * head_dim] = value[:, qkv_width:]


def place_home(blocks, my_place, heads, head_dim):
    rows, width = blocks[0].shape

    def target(at, place):
        return (0, place[0] ^ at)

    return pl.pallas_call(
        functools.partial(home_kernel, heads),
        grid_spec=pltpu.PrefetchScalarGridSpec(
            num_scalar_prefetch=1,
            grid=(PLANE,),
            in_specs=[pl.BlockSpec((rows, width), lambda at, place: (0, 0))] * PLANE,
            out_specs=[
                pl.BlockSpec((rows, heads * 3 * head_dim), target),
                pl.BlockSpec((rows, heads * head_dim), target),
            ],
        ),
        out_shape=[
            jax.ShapeDtypeStruct((rows, PLANE * heads * 3 * head_dim), jnp.float32),
            jax.ShapeDtypeStruct((rows, PLANE * heads * head_dim), jnp.float32),
        ],
        compiler_params=pltpu.CompilerParams(vmem_limit_bytes=32 * 1024 * 1024),
        cost_estimate=pl.CostEstimate(
            flops=PLANE * rows * width,
            bytes_accessed=6 * PLANE * rows * width,
            transcendentals=0,
        ),
        name="place_home",
    )(my_place[None], *blocks)


def per_plane(patches, cotangent, counts, masks, norm_gain, qk_gain, qkv_weight, out_weight):
    replicas = lax.axis_size("fsdp")
    groups = lax.axis_size("tp")
    planes = replicas // PLANE
    my_replica = lax.axis_index("fsdp")
    my_group = lax.axis_index("tp")
    my_plane = my_replica // PLANE
    my_place = lax.rem(my_replica, PLANE)
    tok_rows = patches.shape[0]
    images = counts.shape[1]
    slot_rows = tok_rows // images
    model_width = norm_gain.shape[0]
    share_width = model_width // groups
    head_dim = qk_gain.shape[1]
    shard_rows = qkv_weight.shape[0]
    local_heads = out_weight.shape[1] // head_dim
    heads = local_heads // PLANE
    qkv_width = 3 * head_dim
    head_width = 4 * head_dim
    parts = 2
    slots = images // parts
    part_rows = slots * slot_rows

    replica_ids = jnp.arange(replicas, dtype=jnp.int32)
    relative = jnp.array(ORDER, dtype=jnp.int32)
    own_at = ORDER.index(0)
    sources = (my_replica ^ relative)[:, None] ^ masks[None, :]
    live_counts = jnp.sum(
        jnp.where(replica_ids[:, None, None] == sources[None], counts[:, None, :], 0), axis=0
    ).astype(jnp.int32)
    picks = (relative[:, None] ^ (masks & (PLANE - 1))[None, :]).astype(jnp.int32)
    places = jnp.arange(slot_rows, dtype=jnp.int32)
    is_live = (places[None, :] < live_counts[own_at][:, None]).reshape(tok_rows)

    def by_part(table):
        return jnp.transpose(table).reshape(-1)

    flat_counts = live_counts.reshape(-1)

    holding = lax.dynamic_slice_in_dim(patches, my_group * share_width, share_width, 1)
    holding = holding.reshape(parts, slots, slot_rows, share_width)
    moved = [holding[part] for part in range(parts)]
    first_moved = None
    for bit_place in range(2, replicas.bit_length() - 1):
        previous = None
        for part in range(parts):
            piece = moved[part] if previous is None else after(moved[part], previous)
            partner = swap_fsdp(piece, 2**bit_place)
            moving = jnp.right_shift(masks[part * slots : (part + 1) * slots], bit_place) & 1
            moved[part] = jnp.where((moving == 1)[:, None, None], partner, moved[part])
            previous = partner
            if first_moved is None:
                first_moved = moved[0]
            if part == 0:
                first_there = partner
            if part == 1 and bit_place == 2:
                second_moved = moved[1]

    def head_columns(place):
        qkv_part = lax.dynamic_slice_in_dim(
            qkv_weight, place * heads * qkv_width, heads * qkv_width, 1
        )
        out_part = lax.dynamic_slice_in_dim(
            out_weight, place * heads * head_dim, heads * head_dim, 1
        )
        return jnp.concatenate([qkv_part, out_part], axis=1)

    upstream_own = jnp.where(is_live[:, None], cotangent, jnp.zeros((), cotangent.dtype))
    up_far = [swap_fsdp(upstream_own[:part_rows], 2)]
    up_near = swap_fsdp(after(upstream_own, first_moved), 1)
    shards = spread_places([head_columns(my_place ^ step) for step in range(PLANE)])
    shards = [after(shard, first_moved, up_near, up_far[0]) for shard in shards]
    plane_shard = jnp.zeros((PLANE, shard_rows, heads * head_width), qkv_weight.dtype)
    for step in range(PLANE):
        plane_shard = lax.dynamic_update_index_in_dim(
            plane_shard, shards[step], my_place ^ step, 0
        )
    plane_shard = plane_shard.reshape(PLANE * shard_rows, heads * head_width)
    shards_of = []
    for head in range(heads):
        qkv_at = head * qkv_width
        out_at = heads * qkv_width + head * head_dim
        shard = jnp.concatenate(
            [
                plane_shard[:, qkv_at : qkv_at + qkv_width],
                plane_shard[:, out_at : out_at + head_dim],
            ],
            axis=1,
        )
        shards_of.append(shard)

    gathers = [LineGather(shard, my_plane) for shard in shards_of]
    gathers[0].pair_up(first_there)
    gathers[0].cross(moved[-1])

    here, there = ([], [])
    for part in range(parts):
        own = moved[part]
        over = swap_tp(own)
        if part == 0:
            far = swap_fsdp(after(own, second_moved, *shards), 2)
            far_over = swap_tp(far)
        else:
            far = swap_fsdp(after(own, gathers[0].partner), 2)
            far_over = swap_tp(after(far, over, here[0]))
            pair_up_both(gathers[1], gathers[2], gathers[0].partner)
            up_far.append(swap_fsdp(after(upstream_own[part_rows:], far), 2))
            own = after(own, gathers[0].crossed, gathers[1].partner)
        here.append(
            jnp.stack([own, over, far, far_over]).reshape(
                2, 2, slots, slot_rows, share_width
            )
        )
        there.append(swap_fsdp(here[part], 1))
    gathers[0].spread()
    gathers[1].cross()

    normed, stats = norm_block(
        here,
        there,
        by_part(picks),
        by_part(live_counts),
        norm_gain,
        my_group,
    )
    gathers[1].spread(normed)
    gathers[2].cross(normed)
    up_far[1] = after(up_far[1], normed)
    up_both = [swap_fsdp(after(up_far[0], normed), 1), swap_fsdp(up_far[1], 1)]
    upstream = jnp.concatenate([up_near, *up_both, upstream_own, *up_far])

    scales = jnp.concatenate([qk_gain[0:1] * head_dim ** (-0.5), qk_gain[1:2]])
    weights, mixed_parts, back_parts, reduces = ([], [], [], [])
    for head in range(heads):
        if head == 0:
            weight = gathers[0].whole(normed, gathers[1].crossed, gathers[2].partner)
        elif head == 1:
            weight = gathers[1].whole(qkv_term, out_term, gathers[2].crossed)
            gathers[2].spread(qkv_term)
        else:
            weight = gathers[2].whole(qkv_term, out_term, reduces[0].cross_sent)
        weights.append(weight)
        grad_mixed = mm(upstream, weight[:, qkv_width:], 1, 0).astype(jnp.bfloat16)
        projected = mm(normed, weight[:, :qkv_width], 1, 0)
        mixed, back = attend(projected, grad_mixed, scales, flat_counts, slot_rows)
        mixed_parts.append(mixed)
        back_parts.append(back)
        held_back, held_mixed = (back, mixed)
        if head == 2:
            mixed_all = after(
                jnp.concatenate(mixed_parts, axis=1), reduces[1].arrived, reduces[0].crossed
            )
            out_all = jnp.concatenate([weight[:, qkv_width:] for weight in weights], axis=1)
            out_sent = mm(mixed_all[: 2 * tok_rows], out_all, 1, 1).astype(jnp.bfloat16)
            out_scatter = PlaneScatter(
                out_sent.reshape(2, tok_rows, model_width), share_width, my_group
            )
            reduces[1].add_far(out_sent)
            reduces[1].cross()
            held = after(mixed_all[2 * tok_rows :], out_sent, reduces[1].cross_sent)
            out_kept = mm(held, out_all, 1, 1).astype(jnp.bfloat16)
            held_back = after(held_back, out_kept)
            held_mixed = after(held_mixed, out_kept)
        qkv_term = mm(held_back, normed, 0, 0).astype(jnp.bfloat16)
        out_term = mm(held_mixed, upstream, 0, 0).astype(jnp.bfloat16)
        if head == 1:
            reduces[0].add_far(qkv_term, out_term)
            reduces[0].cross()
        reduces.append(LineReduce([qkv_term, out_term], my_plane))
        reduces[head].inward()

    def send_home(total):
        count = total.shape[0] // head_width
        summed = total.T.reshape(PLANE, shard_rows, count * head_width)
        return spread_places(
            [
                lax.dynamic_index_in_dim(summed, my_place ^ step, 0, keepdims=False)
                for step in range(PLANE)
            ]
        )

    back_all = jnp.concatenate(back_parts, axis=1)
    qkv_all = jnp.concatenate([weight[:, :qkv_width] for weight in weights], axis=1)
    out_added = out_scatter.add_cores(
        after(out_kept.reshape(2, tok_rows, model_width), qkv_term, out_term)
    )
    held = after(back_all[: 2 * tok_rows], *out_added, reduces[2].sent)
    back_sent = mm(held, qkv_all, 1, 1).astype(jnp.bfloat16)
    reduces[2].add_far(back_sent)
    early = PairReduce(reduces[:2], my_plane, back_sent)
    between = (reduces[2].cross_sent, early.sent)
    back_scatter = PlaneScatter(
        after(
            back_sent.reshape(2, tok_rows, model_width),
            out_scatter.over_x,
            out_scatter.over_y,
            *between,
        ),
        share_width,
        my_group,
    )
    turned = out_scatter.turn(*between)
    reduces[2].cross(*turned)
    early.send(*turned)
    held = after(back_all[2 * tok_rows :], *turned, reduces[2].cross_sent)
    back_kept = mm(held, qkv_all, 1, 1).astype(jnp.bfloat16)
    back_added = back_scatter.add_cores(
        after(
            back_kept.reshape(2, tok_rows, model_width),
            out_scatter.last_x,
            out_scatter.last_y,
        )
    )
    late = PairReduce(reduces[2:], my_plane, *back_added)
    late.send()
    turned = back_scatter.turn(late.sent)
    total = jnp.concatenate([early.total(*turned), late.total(*turned)])
    home = send_home(after(total, *turned))
    attended = out_scatter.total()
    attended = jnp.where(is_live[:, None], attended, 0.0).astype(jnp.bfloat16)
    grad_normed = back_scatter.total()

    def own_slot(part, slot):
        pick = picks[own_at, part * slots + slot]
        mine = lax.dynamic_index_in_dim(here[part][:, 0, slot], pick >> 1, 0, keepdims=False)
        other = lax.dynamic_index_in_dim(there[part][:, 0, slot], pick >> 1, 0, keepdims=False)
        return jnp.where((pick & 1) == 1, other, mine)

    own_rows = jnp.concatenate(
        [own_slot(part, slot) for part in range(parts) for slot in range(slots)]
    ).astype(jnp.float32)
    own_rows = jnp.where(is_live[:, None], own_rows, 0.0)
    own_stats = stats[own_at * tok_rows : (own_at + 1) * tok_rows, 0:2]
    mean = own_stats[:, 0:1]
    factor = own_stats[:, 1:2]
    centred = (own_rows - mean) * factor
    gain_share = lax.dynamic_slice_in_dim(norm_gain, my_group * share_width, share_width, 0)
    weighted = grad_normed * gain_share
    sums = jnp.stack([jnp.sum(weighted, axis=-1), jnp.sum(weighted * centred, axis=-1)])
    sums = (sums + swap_tp(sums)) / model_width
    grad_rows = factor * (weighted - sums[0][:, None] - centred * sums[1][:, None])
    grad_rows = grad_rows.astype(jnp.bfloat16)

    grad_qkv_weight, grad_out_weight = place_home(home, my_place, heads, head_dim)
    return (attended, grad_rows, grad_qkv_weight, grad_out_weight)


def solution(mesh):
    def body(patches, cotangent, counts, masks, norm_gain, qk_gain, qkv_weight, out_weight):
        replicas = mesh.shape["fsdp"]
        local_heads = out_weight.shape[1] // qk_gain.shape[1]
        planar = (
            mesh.shape["tp"] == 2
            and replicas == 4 * PLANE
            and replicas & (replicas - 1) == 0
            and local_heads == 3 * PLANE
            and qk_gain.shape[1] == 128
            and counts.shape[1] == 4
        )
        plan = per_plane if planar else per_device
        return plan(
            patches, cotangent, counts, masks, norm_gain, qk_gain, qkv_weight, out_weight
        )

    in_specs = (
        P("fsdp", None),
        P("fsdp", None),
        P(),
        P(),
        P(),
        P(),
        P("fsdp", "tp"),
        P("fsdp", "tp"),
    )
    out_specs = (P("fsdp", "tp"), P("fsdp", "tp"), P("fsdp", "tp"), P("fsdp", "tp"))
    return jax.shard_map(
        body, mesh=mesh, in_specs=in_specs, out_specs=out_specs, check_vma=False
    )
```

```python
import functools
import jax
import jax.numpy as jnp
from jax import lax
from jax.experimental import pallas as pl
from jax.experimental.pallas import tpu as pltpu
from jax.sharding import PartitionSpec as P

epsilon = 1e-06
PLANE = 4
ORDER = (1, 3, 0, 2)


def partner_2(value, axis, stride):
    mask = 2**stride
    pairs = [(source, source ^ mask) for source in range(lax.axis_size(axis))]
    return lax.ppermute(value, axis, pairs)


def norm_rows(values):
    row_mean = jnp.mean(values, axis=-1, keepdims=True)
    centred = values - row_mean
    factor = lax.rsqrt(jnp.mean(centred * centred, axis=-1, keepdims=True) + epsilon)
    return (centred * factor, factor)


def norm_back(upstream, normed, factor):
    return factor * (
        upstream
        - jnp.mean(upstream, axis=-1, keepdims=True)
        - normed * jnp.mean(upstream * normed, axis=-1, keepdims=True)
    )


def per_device(patches, cotangent, counts, masks, norm_gain, qk_gain, qkv_weight, out_weight):
    replicas = lax.axis_size("fsdp")
    groups = lax.axis_size("tp")
    my_replica = lax.axis_index("fsdp")
    my_group = lax.axis_index("tp")
    tok_rows = patches.shape[0]
    images = counts.shape[1]
    slot_rows = tok_rows // images
    model_width = norm_gain.shape[0]
    share_width = model_width // groups
    head_dim = qk_gain.shape[1]
    qkv_cols = qkv_weight.shape[1]
    out_cols = out_weight.shape[1]
    local_heads = out_cols // head_dim
    row_slot = jnp.arange(tok_rows, dtype=jnp.int32) // slot_rows
    holding = lax.dynamic_slice_in_dim(patches, my_group * share_width, share_width, 1)
    digit_count = replicas.bit_length() - 1
    digit_order = list(range(digit_count))
    for bit_place in digit_order:
        partner = partner_2(holding, "fsdp", bit_place)
        moving = jnp.bitwise_and(jnp.right_shift(masks, bit_place), 1) == 1
        take_rows = jnp.take(moving, row_slot)
        holding = jnp.where(take_rows[:, None], partner, holding)
    replica_ids = jnp.arange(replicas, dtype=jnp.int32)
    sources = jnp.bitwise_xor(my_replica, masks)
    run_counts = jnp.sum(jnp.where(replica_ids[:, None] == sources[None, :], counts, 0), axis=0)
    places = jnp.arange(slot_rows, dtype=jnp.int32)
    live_slots = places[None, :] < run_counts[:, None]
    is_live = live_slots.reshape(tok_rows)
    allowed = live_slots[:, :, None] & live_slots[:, None, :] | jnp.eye(slot_rows, dtype=bool)[None]
    packed = jnp.where(is_live[:, None], holding, jnp.zeros((), holding.dtype))
    block_rows = lax.all_gather(packed, "tp", axis=1, tiled=True)
    qkv_full, out_full = (
        lax.all_gather(qkv_weight, "fsdp", axis=0, tiled=True),
        lax.all_gather(out_weight, "fsdp", axis=0, tiled=True),
    )
    centred_rows, row_factor = norm_rows(block_rows.astype(jnp.float32))
    normed = (centred_rows * norm_gain).astype(jnp.bfloat16)
    projected = jnp.dot(normed, qkv_full, preferred_element_type=jnp.float32).reshape(
        images, slot_rows, local_heads, 3, head_dim
    )
    query_hat, query_factor = norm_rows(projected[:, :, :, 0])
    key_hat, key_factor = norm_rows(projected[:, :, :, 1])
    query_scale = qk_gain[0] * head_dim ** (-0.5)
    key_scale = qk_gain[1]
    query = (query_hat * query_scale).astype(jnp.bfloat16)
    key_rows = (key_hat * key_scale).astype(jnp.bfloat16)
    values = projected[:, :, :, 2].astype(jnp.bfloat16)
    scores = jnp.einsum("sqhe,skhe->shqk", query, key_rows, preferred_element_type=jnp.float32)
    raised = jnp.where(allowed[:, None], jnp.exp(scores), 0.0)
    attention = raised / jnp.sum(raised, axis=-1, keepdims=True)
    rounded_attention = attention.astype(jnp.bfloat16)
    mixed = jnp.einsum(
        "shqk,skhe->sqhe", rounded_attention, values, preferred_element_type=jnp.float32
    )
    mixed = mixed.astype(jnp.bfloat16).reshape(tok_rows, out_cols)
    partial_value = lax.dot_general(
        mixed, out_full, (((1,), (1,)), ((), ())), preferred_element_type=jnp.float32
    )
    attended = lax.psum_scatter(
        partial_value.astype(jnp.bfloat16), "tp", scatter_dimension=1, tiled=True
    ).astype(jnp.float32)
    attended = jnp.where(is_live[:, None], attended, 0.0).astype(jnp.bfloat16)
    upstream_rows = jnp.where(is_live[:, None], cotangent, jnp.zeros((), cotangent.dtype))
    grad_mixed = jnp.dot(upstream_rows, out_full, preferred_element_type=jnp.float32).astype(
        jnp.bfloat16
    )
    grad_heads = grad_mixed.reshape(images, slot_rows, local_heads, head_dim)
    grad_value = jnp.einsum(
        "shqk,sqhe->skhe", rounded_attention, grad_heads, preferred_element_type=jnp.float32
    )
    grad_attention = jnp.einsum(
        "sqhe,skhe->shqk", grad_heads, values, preferred_element_type=jnp.float32
    )
    grad_scores = attention * (
        grad_attention - jnp.sum(attention * grad_attention, axis=-1, keepdims=True)
    )
    grad_scores = grad_scores.astype(jnp.bfloat16)
    grad_query = jnp.einsum(
        "shqk,skhe->sqhe", grad_scores, key_rows, preferred_element_type=jnp.float32
    )
    grad_key = jnp.einsum("shqk,sqhe->skhe", grad_scores, query, preferred_element_type=jnp.float32)
    query_grad = norm_back(grad_query * query_scale, query_hat, query_factor)
    key_grad = norm_back(grad_key * key_scale, key_hat, key_factor)
    grad_qkv = (
        jnp.stack([query_grad, key_grad, grad_value], axis=3)
        .astype(jnp.bfloat16)
        .reshape(tok_rows, qkv_cols)
    )
    qkv_term = lax.dot_general(
        normed, grad_qkv, (((0,), (0,)), ((), ())), preferred_element_type=jnp.float32
    )
    out_term = lax.dot_general(
        upstream_rows, mixed, (((0,), (0,)), ((), ())), preferred_element_type=jnp.float32
    )
    stacked = lax.psum_scatter(
        jnp.concatenate([qkv_term, out_term], axis=1).astype(jnp.bfloat16),
        "fsdp",
        scatter_dimension=0,
        tiled=True,
    ).astype(jnp.float32)
    grad_qkv_weight = stacked[:, :qkv_cols]
    grad_out_weight = stacked[:, qkv_cols:]
    partial_back = lax.dot_general(
        grad_qkv, qkv_full, (((1,), (1,)), ((), ())), preferred_element_type=jnp.float32
    )
    summed = lax.psum(partial_back.astype(jnp.bfloat16), "tp").astype(jnp.float32)
    grad_full = norm_back(summed * norm_gain, centred_rows, row_factor)
    grad_share = lax.dynamic_slice_in_dim(grad_full, my_group * share_width, share_width, 1)
    grad_rows = grad_share.astype(jnp.bfloat16)
    return (attended, grad_rows, grad_qkv_weight, grad_out_weight)


def swap_fsdp(value, mask):
    pairs = [(source, source ^ mask) for source in range(lax.axis_size("fsdp"))]
    return lax.ppermute(value, "fsdp", pairs)


def swap_tp(value):
    return lax.ppermute(value, "tp", [(0, 1), (1, 0)])


def send_planes(value, plane_pairs):
    pairs = [
        (source * PLANE + place, target * PLANE + place)
        for source, target in plane_pairs
        for place in range(PLANE)
    ]
    return lax.ppermute(value, "fsdp", pairs)


def after(value, *earlier):
    return lax.optimization_barrier((value,) + earlier)[0]


def spread_places(blocks):
    near = swap_fsdp(jnp.stack([blocks[1], blocks[3]]), 1)
    far = swap_fsdp(jnp.stack([blocks[2], near[1]]), 2)
    return [blocks[0], near[0], far[0], far[1]]


class LineGather:
    def __init__(self, own, my_plane):
        self.own, self.my_plane = (own, my_plane)

    def pair_up(self, *earlier):
        self.partner = swap_fsdp(after(self.own, *earlier), PLANE)

    def cross(self, *earlier):
        even = self.my_plane % 2 == 0
        partner = after(self.partner, *earlier)
        low = jnp.where(even, self.own, partner)
        high = jnp.where(even, partner, self.own)
        self.pair = jnp.concatenate([low, high])
        self.crossed = send_planes(self.pair, [(1, 2), (2, 1)])

    def spread(self, *earlier):
        self.outer = send_planes(after(self.crossed, *earlier), [(1, 0), (2, 3)])

    def whole(self, *earlier):
        inner = (self.my_plane == 1) | (self.my_plane == 2)
        crossed, outer = lax.optimization_barrier((self.crossed, self.outer) + earlier)[:2]
        other = jnp.where(inner, crossed, outer)
        low = self.my_plane < 2
        return jnp.concatenate([jnp.where(low, self.pair, other), jnp.where(low, other, self.pair)])


def pair_up_both(first, second, *earlier):
    both = after(jnp.stack([first.own, second.own]), *earlier)
    both = swap_fsdp(both, PLANE)
    first.partner, second.partner = (both[0], both[1])


def add_rounded(left, right):
    return (left.astype(jnp.float32) + right.astype(jnp.float32)).astype(jnp.bfloat16)


class LineReduce:
    def __init__(self, terms, my_plane):
        self.terms, self.my_plane = (terms, my_plane)
        self.rows = terms[0].shape[1] // 4
        self.far = 2 - 2 * (my_plane // 2)

    def columns(self, start, count):
        return jnp.concatenate(
            [
                lax.dynamic_slice_in_dim(term, start * self.rows, count * self.rows, 1)
                for term in self.terms
            ]
        )

    def inward(self):
        self.sent = self.columns(self.far, 2)
        self.arrived = send_planes(self.sent, [(0, 1), (3, 2)])

    def add_far(self, *earlier):
        far = add_rounded(self.columns(self.far, 2), after(self.arrived, *earlier))
        self.cross_sent = far

    def cross(self, *earlier):
        self.crossed = send_planes(after(self.cross_sent, *earlier), [(1, 2), (2, 1)])

    def of_pair(self, plane, *earlier):
        crossed = after(self.crossed, *earlier)
        crossed = lax.dynamic_slice_in_dim(crossed, plane % 2 * self.rows, self.rows, 1)
        return self.columns(plane, 1).astype(jnp.float32) + crossed.astype(jnp.float32)


class PairReduce:
    def __init__(self, reduces, my_plane, *earlier):
        self.reduces, self.my_plane = (reduces, my_plane)
        sent = jnp.concatenate([reduce.of_pair(my_plane ^ 1, *earlier) for reduce in reduces])
        self.sent = sent.astype(jnp.bfloat16)

    def send(self, *earlier):
        self.got = swap_fsdp(after(self.sent, *earlier), PLANE)

    def total(self, *later):
        kept = [reduce.of_pair(self.my_plane, *later) for reduce in self.reduces]
        got = after(self.got, *later).astype(jnp.float32)
        return (jnp.concatenate(kept) + got).astype(jnp.bfloat16)


def rows_kernel(parts, pick_ref, count_ref, *refs):
    sources, (gain_ref, normed_ref, stats_ref) = (refs[:-3], refs[-3:])
    at = pl.program_id(0)
    rows, half = sources[0].shape[3:]
    width = 2 * half
    live = lax.broadcasted_iota(jnp.int32, (rows, 1), 0) < count_ref[at]
    near = (pick_ref[at] & 1) == 1
    part = at // (pl.num_programs(0) // parts)

    def read(high):
        value = None
        for index in range(parts):
            here, there = sources[4 * index + high], sources[4 * index + 2 + high]
            chosen = jnp.where(near, there[0, 0, 0], here[0, 0, 0])
            value = chosen if value is None else jnp.where(part == index, chosen, value)
        return jnp.where(live, value.astype(jnp.float32), 0.0)

    low = read(0)
    high = read(1)
    mean = (
        jnp.sum(low, axis=-1, keepdims=True) + jnp.sum(high, axis=-1, keepdims=True)
    ) / width
    low = low - mean
    high = high - mean
    variance = (
        jnp.sum(low * low, axis=-1, keepdims=True) + jnp.sum(high * high, axis=-1, keepdims=True)
    ) / width
    factor = lax.rsqrt(variance + epsilon)
    normed_ref[:, :half] = (low * factor * gain_ref[:, :half]).astype(normed_ref.dtype)
    normed_ref[:, half:] = (high * factor * gain_ref[:, half:]).astype(normed_ref.dtype)
    lane = lax.broadcasted_iota(jnp.int32, (rows, stats_ref.shape[1]), 1)
    stats_ref[...] = jnp.where(lane == 0, mean, factor)


def norm_block(here, there, picks, live_counts, norm_gain, my_group):
    parts = len(here)
    _, _, slots, rows, half = here[0].shape
    width = 2 * half
    steps = PLANE * slots
    total = parts * steps
    picks = jnp.concatenate([picks, my_group[None]])

    def source(part, group_xor, near):
        def index(at, pick, count):
            at = jnp.clip(at, part * steps, part * steps + steps - 1)
            first = at // PLANE * PLANE
            stand_in = jnp.where(at - first < 2, first + 2, first + 1)
            chosen = pick[jnp.where((pick[at] & 1) == near, at, stand_in)]
            return (chosen >> 1, pick[total] ^ group_xor, at // PLANE % slots, 0, 0)

        return pl.BlockSpec((1, 1, 1, rows, half), index)

    def target(at, pick, count):
        slot, place = (at // PLANE, at % PLANE)
        return (place * parts * slots + slot, 0)

    arrays, specs = ([], [])
    for part in range(parts):
        arrays += [here[part], here[part], there[part], there[part]]
        specs += [source(part, 0, 0), source(part, 1, 0), source(part, 0, 1), source(part, 1, 1)]
    return pl.pallas_call(
        functools.partial(rows_kernel, parts),
        grid_spec=pltpu.PrefetchScalarGridSpec(
            num_scalar_prefetch=2,
            grid=(total,),
            in_specs=specs + [pl.BlockSpec((1, width), lambda at, pick, count: (0, 0))],
            out_specs=[pl.BlockSpec((rows, width), target), pl.BlockSpec((rows, 128), target)],
        ),
        out_shape=[
            jax.ShapeDtypeStruct((total * rows, width), jnp.bfloat16),
            jax.ShapeDtypeStruct((total * rows, 128), jnp.float32),
        ],
        compiler_params=pltpu.CompilerParams(vmem_limit_bytes=28 * 1024 * 1024),
        cost_estimate=pl.CostEstimate(
            flops=10 * total * rows * width,
            bytes_accessed=6 * total * rows * width,
            transcendentals=0,
        ),
        name="norm_rows",
    )(picks, live_counts, *arrays, norm_gain[None, :])


def mm(left, right, left_dim, right_dim):
    return lax.dot_general(
        left,
        right,
        (((left_dim,), (right_dim,)), ((), ())),
        preferred_element_type=jnp.float32,
    )


def attend_image(projected, grad_mixed, scales, live, rows, head_dim):
    query_hat, query_factor = norm_rows(projected[:, :head_dim])
    key_hat, key_factor = norm_rows(projected[:, head_dim : 2 * head_dim])
    query_scale = scales[0:1, :]
    key_scale = scales[1:2, :]
    query = (query_hat * query_scale).astype(jnp.bfloat16)
    key_rows = (key_hat * key_scale).astype(jnp.bfloat16)
    values = projected[:, 2 * head_dim :].astype(jnp.bfloat16)
    row_id = lax.broadcasted_iota(jnp.int32, (rows, rows), 0)
    col_id = lax.broadcasted_iota(jnp.int32, (rows, rows), 1)
    allowed = ((row_id < live) & (col_id < live)) | (row_id == col_id)
    raised = jnp.where(allowed, jnp.exp(mm(query, key_rows, 1, 1)), 0.0)
    attention = raised / jnp.sum(raised, axis=-1, keepdims=True)
    rounded = attention.astype(jnp.bfloat16)
    mixed = mm(rounded, values, 1, 0).astype(jnp.bfloat16)
    grad_value = mm(rounded, grad_mixed, 0, 0)
    grad_attention = mm(grad_mixed, values, 1, 1)
    grad_scores = attention * (
        grad_attention - jnp.sum(attention * grad_attention, axis=-1, keepdims=True)
    )
    grad_scores = grad_scores.astype(jnp.bfloat16)
    grad_query = mm(grad_scores, key_rows, 1, 0)
    grad_key = mm(grad_scores, query, 0, 0)
    query_grad = norm_back(grad_query * query_scale, query_hat, query_factor)
    key_grad = norm_back(grad_key * key_scale, key_hat, key_factor)
    return (mixed, query_grad, key_grad, grad_value)


def attention_kernel(per_step, count_ref, proj_ref, grad_ref, scale_ref, mixed_ref, back_ref):
    at = pl.program_id(0)
    rows = proj_ref.shape[0] // per_step
    head_dim = grad_ref.shape[1]
    scales = scale_ref[...]
    for image in range(per_step):
        span = slice(image * rows, (image + 1) * rows)
        mixed, query_grad, key_grad, grad_value = attend_image(
            proj_ref[span, :],
            grad_ref[span, :],
            scales,
            count_ref[at * per_step + image],
            rows,
            head_dim,
        )
        mixed_ref[span, :] = mixed
        back_ref[span, :head_dim] = query_grad.astype(jnp.bfloat16)
        back_ref[span, head_dim : 2 * head_dim] = key_grad.astype(jnp.bfloat16)
        back_ref[span, 2 * head_dim :] = grad_value.astype(jnp.bfloat16)


def attend(projected, grad_mixed, scales, live_counts, rows):
    total, head_dim = grad_mixed.shape
    image_count = total // rows
    per_step = 4
    block = per_step * rows
    return pl.pallas_call(
        functools.partial(attention_kernel, per_step),
        grid_spec=pltpu.PrefetchScalarGridSpec(
            num_scalar_prefetch=1,
            grid=(image_count // per_step,),
            in_specs=[
                pl.BlockSpec((block, 3 * head_dim), lambda at, count: (at, 0)),
                pl.BlockSpec((block, head_dim), lambda at, count: (at, 0)),
                pl.BlockSpec((2, head_dim), lambda at, count: (0, 0)),
            ],
            out_specs=[
                pl.BlockSpec((block, head_dim), lambda at, count: (at, 0)),
                pl.BlockSpec((block, 3 * head_dim), lambda at, count: (at, 0)),
            ],
        ),
        out_shape=[
            jax.ShapeDtypeStruct((total, head_dim), jnp.bfloat16),
            jax.ShapeDtypeStruct((total, 3 * head_dim), jnp.bfloat16),
        ],
        compiler_params=pltpu.CompilerParams(vmem_limit_bytes=32 * 1024 * 1024),
        cost_estimate=pl.CostEstimate(
            flops=12 * total * rows * head_dim,
            bytes_accessed=12 * total * head_dim * 2,
            transcendentals=total * rows,
        ),
        name="attend_images",
    )(live_counts, projected, grad_mixed, scales)


class PlaneScatter:
    def __init__(self, sent, share_width, my_group):
        self.share_width, self.my_group = (share_width, my_group)
        self.got = swap_fsdp(sent, 1)

    def mine(self, value):
        start = self.my_group * self.share_width
        return lax.dynamic_slice_in_dim(value, start, self.share_width, value.ndim - 1)

    def other(self, value):
        start = (1 - self.my_group) * self.share_width
        return lax.dynamic_slice_in_dim(value, start, self.share_width, value.ndim - 1)

    def add_cores(self, kept, *earlier):
        got = after(self.got, *earlier) if earlier else self.got
        half = kept.shape[1] // 2
        first = add_rounded(kept[:, :half], got[:, :half])
        near = add_rounded(kept[0, half:], got[0, half:])
        far = add_rounded(kept[1, half:], got[1, half:])
        self.first, self.near = (first, near)
        sent_x = self.other(first)
        self.over_x = swap_tp(sent_x)
        self.over_y = swap_fsdp(far, 2)
        return (first, far, sent_x)

    def turn(self, *earlier):
        over_x = after(self.over_x, *earlier)
        over_y = after(self.over_y, *earlier)
        first = self.mine(self.first).astype(jnp.float32) + over_x.astype(jnp.float32)
        second = self.near.astype(jnp.float32) + over_y.astype(jnp.float32)
        self.first_sum = first[0]
        self.second_sum = self.mine(second)
        sent_y = first[1].astype(jnp.bfloat16)
        sent_x = self.other(second).astype(jnp.bfloat16)
        self.last_y = swap_fsdp(sent_y, 2)
        self.last_x = swap_tp(sent_x)
        return (sent_y, sent_x)

    def total(self):
        return jnp.concatenate(
            [
                self.first_sum + self.last_y.astype(jnp.float32),
                self.second_sum + self.last_x.astype(jnp.float32),
            ]
        )


def home_kernel(heads, place_ref, *refs):
    block_refs, (qkv_ref, out_ref) = (refs[:PLANE], refs[-2:])
    at = pl.program_id(0)
    qkv_width = qkv_ref.shape[1] // heads
    head_dim = out_ref.shape[1] // heads
    head_width = qkv_width + head_dim
    for step in range(PLANE):

        @pl.when(at == step)
        def _():
            for head in range(heads):
                low = head * head_width
                value = block_refs[step][:, low : low + head_width].astype(jnp.float32)
                qkv_ref[:, head * qkv_width : (head + 1) * qkv_width] = value[:, :qkv_width]
                out_ref[:, head * head_dim : (head + 1) * head_dim] = value[:, qkv_width:]


def place_home(blocks, my_place, heads, head_dim):
    rows, width = blocks[0].shape

    def target(at, place):
        return (0, place[0] ^ at)

    return pl.pallas_call(
        functools.partial(home_kernel, heads),
        grid_spec=pltpu.PrefetchScalarGridSpec(
            num_scalar_prefetch=1,
            grid=(PLANE,),
            in_specs=[pl.BlockSpec((rows, width), lambda at, place: (0, 0))] * PLANE,
            out_specs=[
                pl.BlockSpec((rows, heads * 3 * head_dim), target),
                pl.BlockSpec((rows, heads * head_dim), target),
            ],
        ),
        out_shape=[
            jax.ShapeDtypeStruct((rows, PLANE * heads * 3 * head_dim), jnp.float32),
            jax.ShapeDtypeStruct((rows, PLANE * heads * head_dim), jnp.float32),
        ],
        compiler_params=pltpu.CompilerParams(vmem_limit_bytes=32 * 1024 * 1024),
        cost_estimate=pl.CostEstimate(
            flops=PLANE * rows * width,
            bytes_accessed=6 * PLANE * rows * width,
            transcendentals=0,
        ),
        name="place_home",
    )(my_place[None], *blocks)


def per_plane(patches, cotangent, counts, masks, norm_gain, qk_gain, qkv_weight, out_weight):
    replicas = lax.axis_size("fsdp")
    groups = lax.axis_size("tp")
    planes = replicas // PLANE
    my_replica = lax.axis_index("fsdp")
    my_group = lax.axis_index("tp")
    my_plane = my_replica // PLANE
    my_place = lax.rem(my_replica, PLANE)
    tok_rows = patches.shape[0]
    images = counts.shape[1]
    slot_rows = tok_rows // images
    model_width = norm_gain.shape[0]
    share_width = model_width // groups
    head_dim = qk_gain.shape[1]
    shard_rows = qkv_weight.shape[0]
    local_heads = out_weight.shape[1] // head_dim
    heads = local_heads // PLANE
    qkv_width = 3 * head_dim
    head_width = 4 * head_dim
    parts = 2
    slots = images // parts
    part_rows = slots * slot_rows

    replica_ids = jnp.arange(replicas, dtype=jnp.int32)
    relative = jnp.array(ORDER, dtype=jnp.int32)
    own_at = ORDER.index(0)
    sources = (my_replica ^ relative)[:, None] ^ masks[None, :]
    live_counts = jnp.sum(
        jnp.where(replica_ids[:, None, None] == sources[None], counts[:, None, :], 0), axis=0
    ).astype(jnp.int32)
    picks = (relative[:, None] ^ (masks & (PLANE - 1))[None, :]).astype(jnp.int32)
    places = jnp.arange(slot_rows, dtype=jnp.int32)
    is_live = (places[None, :] < live_counts[own_at][:, None]).reshape(tok_rows)

    def by_part(table):
        return jnp.transpose(table).reshape(-1)

    flat_counts = live_counts.reshape(-1)

    holding = lax.dynamic_slice_in_dim(patches, my_group * share_width, share_width, 1)
    holding = holding.reshape(parts, slots, slot_rows, share_width)
    moved = [holding[part] for part in range(parts)]
    first_moved = None
    for bit_place in range(2, replicas.bit_length() - 1):
        previous = None
        for part in range(parts):
            piece = moved[part] if previous is None else after(moved[part], previous)
            partner = swap_fsdp(piece, 2**bit_place)
            moving = jnp.right_shift(masks[part * slots : (part + 1) * slots], bit_place) & 1
            moved[part] = jnp.where((moving == 1)[:, None, None], partner, moved[part])
            previous = partner
            if first_moved is None:
                first_moved = moved[0]
            if part == 0:
                first_there = partner
            if part == 1 and bit_place == 2:
                second_moved = moved[1]

    def head_columns(place):
        qkv_part = lax.dynamic_slice_in_dim(
            qkv_weight, place * heads * qkv_width, heads * qkv_width, 1
        )
        out_part = lax.dynamic_slice_in_dim(
            out_weight, place * heads * head_dim, heads * head_dim, 1
        )
        return jnp.concatenate([qkv_part, out_part], axis=1)

    upstream_own = jnp.where(is_live[:, None], cotangent, jnp.zeros((), cotangent.dtype))
    up_far = [swap_fsdp(upstream_own[:part_rows], 2)]
    up_near = swap_fsdp(after(upstream_own, first_moved), 1)
    shards = spread_places([head_columns(my_place ^ step) for step in range(PLANE)])
    shards = [after(shard, first_moved, up_near, up_far[0]) for shard in shards]
    plane_shard = jnp.zeros((PLANE, shard_rows, heads * head_width), qkv_weight.dtype)
    for step in range(PLANE):
        plane_shard = lax.dynamic_update_index_in_dim(
            plane_shard, shards[step], my_place ^ step, 0
        )
    plane_shard = plane_shard.reshape(PLANE * shard_rows, heads * head_width)
    shards_of = []
    for head in range(heads):
        qkv_at = head * qkv_width
        out_at = heads * qkv_width + head * head_dim
        shard = jnp.concatenate(
            [
                plane_shard[:, qkv_at : qkv_at + qkv_width],
                plane_shard[:, out_at : out_at + head_dim],
            ],
            axis=1,
        )
        shards_of.append(shard)

    gathers = [LineGather(shard, my_plane) for shard in shards_of]
    gathers[0].pair_up(first_there)
    gathers[0].cross(moved[-1])

    here, there = ([], [])
    for part in range(parts):
        own = moved[part]
        over = swap_tp(own)
        if part == 0:
            far = swap_fsdp(after(own, second_moved, *shards), 2)
            far_over = swap_tp(far)
        else:
            far = swap_fsdp(after(own, gathers[0].partner), 2)
            far_over = swap_tp(after(far, over, here[0]))
            pair_up_both(gathers[1], gathers[2], gathers[0].partner)
            up_far.append(swap_fsdp(after(upstream_own[part_rows:], far), 2))
            own = after(own, gathers[0].crossed, gathers[1].partner)
        here.append(
            jnp.stack([own, over, far, far_over]).reshape(
                2, 2, slots, slot_rows, share_width
            )
        )
        there.append(swap_fsdp(here[part], 1))
    gathers[0].spread()
    gathers[1].cross()

    normed, stats = norm_block(
        here,
        there,
        by_part(picks),
        by_part(live_counts),
        norm_gain,
        my_group,
    )
    gathers[1].spread(normed)
    gathers[2].cross(normed)
    up_far[1] = after(up_far[1], normed)
    up_both = [swap_fsdp(after(up_far[0], normed), 1), swap_fsdp(up_far[1], 1)]
    upstream = jnp.concatenate([up_near, *up_both, upstream_own, *up_far])

    scales = jnp.concatenate([qk_gain[0:1] * head_dim ** (-0.5), qk_gain[1:2]])
    weights, mixed_parts, back_parts, reduces = ([], [], [], [])
    for head in range(heads):
        if head == 0:
            weight = gathers[0].whole(normed, gathers[1].crossed, gathers[2].partner)
        elif head == 1:
            weight = gathers[1].whole(qkv_term, out_term, gathers[2].crossed)
            gathers[2].spread(qkv_term)
        else:
            weight = gathers[2].whole(qkv_term, out_term, reduces[0].cross_sent)
        weights.append(weight)
        grad_mixed = mm(upstream, weight[:, qkv_width:], 1, 0).astype(jnp.bfloat16)
        projected = mm(normed, weight[:, :qkv_width], 1, 0)
        mixed, back = attend(projected, grad_mixed, scales, flat_counts, slot_rows)
        mixed_parts.append(mixed)
        back_parts.append(back)
        held_back, held_mixed = (back, mixed)
        if head == 2:
            mixed_all = after(
                jnp.concatenate(mixed_parts, axis=1), reduces[1].arrived, reduces[0].crossed
            )
            out_all = jnp.concatenate([weight[:, qkv_width:] for weight in weights], axis=1)
            out_sent = mm(mixed_all[: 2 * tok_rows], out_all, 1, 1).astype(jnp.bfloat16)
            out_scatter = PlaneScatter(
                out_sent.reshape(2, tok_rows, model_width), share_width, my_group
            )
            reduces[1].add_far(out_sent)
            reduces[1].cross()
            held = after(mixed_all[2 * tok_rows :], out_sent, reduces[1].cross_sent)
            out_kept = mm(held, out_all, 1, 1).astype(jnp.bfloat16)
            held_back = after(held_back, out_kept)
            held_mixed = after(held_mixed, out_kept)
        qkv_term = mm(held_back, normed, 0, 0).astype(jnp.bfloat16)
        out_term = mm(held_mixed, upstream, 0, 0).astype(jnp.bfloat16)
        if head == 1:
            reduces[0].add_far(qkv_term, out_term)
            reduces[0].cross()
        reduces.append(LineReduce([qkv_term, out_term], my_plane))
        reduces[head].inward()

    def send_home(total):
        count = total.shape[0] // head_width
        summed = total.T.reshape(PLANE, shard_rows, count * head_width)
        return spread_places(
            [
                lax.dynamic_index_in_dim(summed, my_place ^ step, 0, keepdims=False)
                for step in range(PLANE)
            ]
        )

    back_all = jnp.concatenate(back_parts, axis=1)
    qkv_all = jnp.concatenate([weight[:, :qkv_width] for weight in weights], axis=1)
    out_added = out_scatter.add_cores(
        after(out_kept.reshape(2, tok_rows, model_width), qkv_term, out_term)
    )
    held = after(back_all[: 2 * tok_rows], *out_added, reduces[2].sent)
    back_sent = mm(held, qkv_all, 1, 1).astype(jnp.bfloat16)
    reduces[2].add_far(back_sent)
    early = PairReduce(reduces[:2], my_plane, back_sent)
    between = (reduces[2].cross_sent, early.sent)
    back_scatter = PlaneScatter(
        after(
            back_sent.reshape(2, tok_rows, model_width),
            out_scatter.over_x,
            out_scatter.over_y,
            *between,
        ),
        share_width,
        my_group,
    )
    turned = out_scatter.turn(*between)
    reduces[2].cross(*turned)
    early.send(*turned)
    held = after(back_all[2 * tok_rows :], *turned, reduces[2].cross_sent)
    back_kept = mm(held, qkv_all, 1, 1).astype(jnp.bfloat16)
    back_added = back_scatter.add_cores(
        after(
            back_kept.reshape(2, tok_rows, model_width),
            out_scatter.last_x,
            out_scatter.last_y,
        )
    )
    late = PairReduce(reduces[2:], my_plane, *back_added)
    late.send()
    turned = back_scatter.turn(late.sent)
    early_home = send_home(after(early.total(*turned), *turned))
    late_home = send_home(late.total(*turned, early_home[1]))
    home = [jnp.concatenate(pair, axis=1) for pair in zip(early_home, late_home)]
    attended = out_scatter.total()
    attended = jnp.where(is_live[:, None], attended, 0.0).astype(jnp.bfloat16)
    grad_normed = back_scatter.total()

    def own_slot(part, slot):
        pick = picks[own_at, part * slots + slot]
        mine = lax.dynamic_index_in_dim(here[part][:, 0, slot], pick >> 1, 0, keepdims=False)
        other = lax.dynamic_index_in_dim(there[part][:, 0, slot], pick >> 1, 0, keepdims=False)
        return jnp.where((pick & 1) == 1, other, mine)

    own_rows = jnp.concatenate(
        [own_slot(part, slot) for part in range(parts) for slot in range(slots)]
    ).astype(jnp.float32)
    own_rows = jnp.where(is_live[:, None], own_rows, 0.0)
    own_stats = stats[own_at * tok_rows : (own_at + 1) * tok_rows, 0:2]
    mean = own_stats[:, 0:1]
    factor = own_stats[:, 1:2]
    centred = (own_rows - mean) * factor
    gain_share = lax.dynamic_slice_in_dim(norm_gain, my_group * share_width, share_width, 0)
    weighted = grad_normed * gain_share
    sums = jnp.stack([jnp.sum(weighted, axis=-1), jnp.sum(weighted * centred, axis=-1)])
    sums = (sums + swap_tp(sums)) / model_width
    grad_rows = factor * (weighted - sums[0][:, None] - centred * sums[1][:, None])
    grad_rows = grad_rows.astype(jnp.bfloat16)

    grad_qkv_weight, grad_out_weight = place_home(home, my_place, heads, head_dim)
    return (attended, grad_rows, grad_qkv_weight, grad_out_weight)


def solution(mesh):
    def body(patches, cotangent, counts, masks, norm_gain, qk_gain, qkv_weight, out_weight):
        replicas = mesh.shape["fsdp"]
        local_heads = out_weight.shape[1] // qk_gain.shape[1]
        planar = (
            mesh.shape["tp"] == 2
            and replicas == 4 * PLANE
            and replicas & (replicas - 1) == 0
            and local_heads == 3 * PLANE
            and qk_gain.shape[1] == 128
            and counts.shape[1] == 4
        )
        plan = per_plane if planar else per_device
        return plan(
            patches, cotangent, counts, masks, norm_gain, qk_gain, qkv_weight, out_weight
        )

    in_specs = (
        P("fsdp", None),
        P("fsdp", None),
        P(),
        P(),
        P(),
        P(),
        P("fsdp", "tp"),
        P("fsdp", "tp"),
    )
    out_specs = (P("fsdp", "tp"), P("fsdp", "tp"), P("fsdp", "tp"), P("fsdp", "tp"))
    return jax.shard_map(
        body, mesh=mesh, in_specs=in_specs, out_specs=out_specs, check_vma=False
    )
```
